32 devices in a mesh: pipe: 16 (over z, y, x), tp: 2 (over core).
Axes of the slice: x: 2, y: 2, z: 4, core: 2. Of those that a mesh axis runs over, the one named last changes fastest.
Arguments:
- hidden: bfloat16 [2, 64, 8192], P(None, None, 'tp'), may hold values from -6 to 6
- rewards: float32 [2, 64], replicated, may hold values from -6 to 6
- counts: int32 [2], replicated, may hold values from 1 to 64, as said below
- episode: int32 [2, 64], replicated, may hold values from 0 to 3, as said below
- down_weight: bfloat16 [16, 8192, 256], P('pipe', 'tp'), may hold values from -0.0625 to 0.0625
- up_weight: bfloat16 [16, 256, 8192], P('pipe', None, 'tp'), may hold values from -0.09375 to 0.09375
- head_weight: bfloat16 [8192], P('tp'), may hold values from -0.03125 to 0.03125
Outputs:
- grad_down: float32 [16, 8192, 256], P('pipe', 'tp')
- grad_up: float32 [16, 256, 8192], P('pipe', None, 'tp')
- grad_head: float32 [2, 4096], P('tp', 'pipe')
- advantages: float32 [2, 64], replicated
The draws below stay inside these ranges and needn't reach their ends.
Inputs may be any that keep to these rules, and one draw needn't show every extreme that they name: Micro-batch m has counts[m] live tokens in its first slots; one micro-batch is full. `episode`: episode ids never fall along a micro-batch; each of the four ids holds 1 to 32 slots of every micro-batch, one of them exactly 32.
All inputs are finite; a program needn't handle non-finite values.
Results may differ from the reference program's by a relative error of at most 0.023.
Values may be sent and summed in bfloat16 or wider, within the bound.
A program may use at most 64 MiB of HBM per device.

```python
import jax
import jax.numpy as jnp
from jax import lax

D = 8192
R = 256
MB = 2
CAP = 64
LAYERS = 16
N_TP = 2


def layout(key):
    count_key, full_key, episode_key, place_key = jax.random.split(key, 4)
    drawn = jax.random.randint(count_key, (MB,), 1, CAP + 1)
    full_index = jax.random.randint(full_key, (), 0, MB)
    counts = jnp.where(jnp.arange(MB) == full_index, CAP, drawn).astype(jnp.int32)
    half_span = CAP // 2

    def cut_points(one_key):
        return jnp.sort(jax.random.permutation(one_key, half_span - 1)[:2] + 1)
    cut_pairs = jax.vmap(cut_points)(jax.random.split(episode_key, MB)).astype(jnp.int32)
    pieces = jnp.stack([cut_pairs[:, 0], cut_pairs[:, 1] - cut_pairs[:, 0], half_span - cut_pairs[:, 1]], axis=1).astype(jnp.int32)
    placed = jax.random.randint(place_key, (MB,), 0, 4).astype(jnp.int32)
    slot_ids = jnp.arange(4, dtype=jnp.int32)
    moved = jnp.clip(slot_ids[None, :] - (slot_ids[None, :] > placed[:, None]).astype(jnp.int32), 0, 2)
    spans = jnp.where(slot_ids[None, :] == placed[:, None], jnp.int32(half_span), jnp.take_along_axis(pieces, moved, axis=1))
    bounds = jnp.cumsum(spans, axis=1).astype(jnp.int32)
    position = jnp.arange(CAP, dtype=jnp.int32)
    episode = jnp.sum((position[None, :, None] >= bounds[:, None, :3]).astype(jnp.int32), axis=2).astype(jnp.int32)
    next_differs = jnp.concatenate([episode[:, 1:] != episode[:, :-1], jnp.ones((MB, 1), jnp.bool_)], axis=1)
    terminal = next_differs | (position[None, :] == counts[:, None] - 1)
    return (counts, episode, terminal)


def draw_counts(key, part):
    shared = layout(key)
    return shared[0]


def draw_episode(key, part):
    shared = layout(key)
    return shared[1]


def draw_rewards(key, part):
    shared = layout(key)
    key = jax.random.fold_in(key, 7)
    sign_key, size_key, noise_key = jax.random.split(key, 3)
    episode = shared[1]
    terminal = shared[2].astype(jnp.float32)
    signs = jnp.where(jax.random.randint(sign_key, (MB, 4), 0, 2) == 1, 1.0, -1.0).astype(jnp.float32)
    sizes = jnp.exp(jax.random.uniform(size_key, (MB, 4), jnp.float32, jnp.log(4.0), jnp.log(5.0)))
    noise = 0.1 * jax.random.normal(noise_key, (MB, CAP), jnp.float32)
    scores = signs * sizes
    slot_score = jnp.sum(jnp.where(episode[:, :, None] == jnp.arange(4, dtype=jnp.int32)[None, None, :], scores[:, None, :], 0.0), axis=2)
    return (noise + terminal * slot_score).astype(jnp.float32)


def level_of(rng, shape, shards, smallest, largest):
    loudness = 1.0
    for dim, shards_of in shards:
        steps = jax.random.uniform(jax.random.fold_in(jax.random.fold_in(rng, 6), dim), (shards_of,), jnp.float32, smallest / len(shards), largest / len(shards))
        loudness = loudness * jnp.repeat(jnp.exp(steps), shape[dim] // shards_of).reshape((-1,) + (1,) * (len(shape) - 1 - dim))
    return loudness


def scatter_about(own_key, dims, scale, most, cuts=(), kind=jnp.bfloat16):
    values = jax.random.normal(own_key, dims, jnp.float32) * scale
    if len(cuts) > 0:
        values = level_of(own_key, dims, cuts, -0.22, 0.18) * values
    return jnp.clip(values, min=-most, max=most).astype(kind)


def setup_inputs(seed: int = 0) -> dict:
    key_of = jax.random.split(jax.random.key(seed), 8)
    hidden = scatter_about(key_of[0], (MB, CAP, D), 1.0, 6.0, ((2, 2),))
    rewards = draw_rewards(jax.random.fold_in(key_of[7], 71), 0)
    counts = draw_counts(jax.random.fold_in(key_of[7], 71), 0)
    episode = draw_episode(jax.random.fold_in(key_of[7], 71), 0)
    down_weight = scatter_about(key_of[4], (LAYERS, D, R), D ** -0.5, 0.0625, ((0, 16), (1, 2)))
    up_weight = scatter_about(key_of[5], (LAYERS, R, D), (16 * R) ** -0.5, 0.09375, ((0, 16), (2, 2)))
    head_weight = scatter_about(key_of[6], (D,), (4 * D) ** -0.5, 0.03125, ((0, 2),))
    return dict(hidden=hidden, rewards=rewards, counts=counts, episode=episode, down_weight=down_weight, up_weight=up_weight, head_weight=head_weight)


DISCOUNT = 1.0
TRACE = 1.0


def derivative(pre_act):
    sigmoid_value = jax.nn.sigmoid(pre_act)
    return sigmoid_value * (1.0 + pre_act * (1.0 - sigmoid_value))


def advantage(values, rewards, counts, episode):
    batch_total = values.shape[0]
    slot_total = values.shape[1]
    position = jnp.arange(slot_total, dtype=jnp.int32)
    live_mask = (position[None, :] < counts[:, None]).astype(jnp.float32)
    next_live = (position[None, :] + 1) < counts[:, None]
    same_next = jnp.concatenate([episode[:, 1:] == episode[:, :-1], jnp.zeros((batch_total, 1), jnp.bool_)], axis=1)
    follow = (next_live & same_next).astype(jnp.float32)
    next_value = jnp.concatenate([values[:, 1:], jnp.zeros((batch_total, 1), jnp.float32)], axis=1)
    deltas = (rewards + DISCOUNT * follow * next_value - values) * live_mask
    later_mask = position[None, :] >= position[:, None]
    distance = jnp.maximum(position[None, :] - position[:, None], 0).astype(jnp.float32)
    decay_table = jnp.power(jnp.float32(TRACE * DISCOUNT), distance)
    same_episode = episode[:, :, None] == episode[:, None, :]
    weights = jnp.where(later_mask[None] & same_episode & (live_mask[:, None, :] > 0), decay_table[None], jnp.float32(0.0))
    return jnp.einsum("mtk,mk->mt", weights, deltas, precision=lax.Precision.HIGHEST) * live_mask


def reference(hidden, rewards, counts, episode, down_weight, up_weight, head_weight):
    flat_rows = hidden.reshape(MB * CAP, D)

    def forward_layer(rows_in, weights):
        down_layer, up_layer = weights
        pre_act = jnp.dot(rows_in, down_layer, preferred_element_type=jnp.float32)
        activated = jax.nn.silu(pre_act).astype(jnp.bfloat16)
        rows_out = (rows_in.astype(jnp.float32) + jnp.dot(activated, up_layer, preferred_element_type=jnp.float32)).astype(jnp.bfloat16)
        return rows_out, (rows_in, pre_act)

    final_rows, (inputs_kept, pre_kept) = lax.scan(forward_layer, flat_rows, (down_weight, up_weight))
    values = jnp.dot(final_rows, head_weight[:, None], preferred_element_type=jnp.float32).reshape(MB, CAP)
    advantages = advantage(values, rewards, counts, episode)
    value_grad = -advantages.reshape(MB * CAP)
    grad_head = jnp.dot(final_rows.astype(jnp.float32).T, value_grad, precision=lax.Precision.HIGHEST)
    grad_final = (value_grad[:, None] * head_weight.astype(jnp.float32)[None, :]).astype(jnp.bfloat16)

    def backward_layer(grad_out, stored):
        down_layer, up_layer, rows_in, pre_act = stored
        summed = jnp.dot(grad_out, up_layer.T, preferred_element_type=jnp.float32)
        pre_grad = (summed * derivative(pre_act)).astype(jnp.bfloat16)
        grad_in = (grad_out.astype(jnp.float32) + jnp.dot(pre_grad, down_layer.T, preferred_element_type=jnp.float32)).astype(jnp.bfloat16)
        activated = jax.nn.silu(pre_act).astype(jnp.bfloat16)
        down_grad = jnp.dot(rows_in.T, pre_grad, preferred_element_type=jnp.float32)
        up_grad = jnp.dot(activated.T, grad_out, preferred_element_type=jnp.float32)
        return grad_in, (down_grad, up_grad)

    unused_grad, (grad_down, grad_up) = lax.scan(backward_layer, grad_final, (down_weight, up_weight, inputs_kept, pre_kept), reverse=True)
    return grad_down, grad_up, grad_head.reshape(N_TP, D // N_TP), advantages
```

```python
import functools

import jax
import jax.numpy as jnp
from jax import lax
from jax.experimental import pallas as pl
from jax.experimental.pallas import tpu as pltpu
from jax.sharding import PartitionSpec as P

MESH = pl.DeviceIdType.MESH
CHUNK = 16
PIECES = 4
NT = (((1,), (1,)), ((), ()))


def derivative(pre_act):
    s = jax.nn.sigmoid(pre_act)
    return s * (1.0 + pre_act * (1.0 - s))


def kernel(
    n_pipe,
    n_tp,
    batch,
    hidden,
    rewards,
    counts,
    episode,
    down,
    up,
    head,
    h_out,
    act_out,
    pg_out,
    g_out,
    msg_out,
    h_buf,
    o_buf,
    g_buf,
    q_buf,
    act_buf,
    pg_buf,
    pre_buf,
    fx,
    bx,
    vx,
    w_buf,
    aux,
    msg,
    msg_in,
    f_send,
    f_recv,
    b_send,
    b_recv,
    fx_send,
    fx_recv,
    bx_send,
    bx_recv,
    vx_send,
    vx_recv,
    msg_send,
    msg_recv,
    local_sem,
):
    p = lax.axis_index("pipe")
    me = lax.axis_index("tp")
    last = n_pipe - 1
    is_last = p == last
    rows, width = h_buf.shape
    inner = down.shape[1]
    chunks = rows // CHUNK
    piece = width // PIECES
    peers = [lax.rem(me + i, n_tp) for i in range(1, n_tp)]
    block = msg.shape[2]

    def to_pipe(q):
        return {"pipe": q, "tp": me}

    def to_peer(t):
        return {"pipe": p, "tp": t}

    barrier = pltpu.get_barrier_semaphore()
    for t in peers:
        pl.semaphore_signal(barrier, inc=1, device_id=to_peer(t), device_id_type=MESH)

    @pl.when(p > 0)
    def _():
        pl.semaphore_signal(barrier, inc=1, device_id=to_pipe(p - 1), device_id_type=MESH)

    @pl.when(p < last)
    def _():
        pl.semaphore_signal(barrier, inc=1, device_id=to_pipe(p + 1), device_id_type=MESH)
        pl.semaphore_signal(barrier, inc=1, device_id=to_pipe(last), device_id_type=MESH)

    @pl.when(is_last)
    def _():
        def greet(q, carry):
            pl.semaphore_signal(barrier, inc=1, device_id=to_pipe(q), device_id_type=MESH)
            return carry

        lax.fori_loop(0, last, greet, 0)

    @pl.when(p == 0)
    def _():
        pl.semaphore_wait(barrier, n_tp + 1)

    @pl.when((p > 0) & (p < last))
    def _():
        pl.semaphore_wait(barrier, n_tp + 2)

    @pl.when(is_last)
    def _():
        pl.semaphore_wait(barrier, n_tp + last)

    @pl.when(p == 0)
    def _():
        copy = pltpu.make_async_copy(hidden, h_buf, local_sem.at[0])
        copy.start()
        copy.wait()

    @pl.when(is_last)
    def _():
        shape = (rows, rows)
        i = lax.broadcasted_iota(jnp.int32, shape, 0)
        j = lax.broadcasted_iota(jnp.int32, shape, 1)
        cap = rows // batch

        def per_slot(idx):
            live = jnp.zeros(shape, jnp.float32)
            next_live = jnp.zeros(shape, jnp.float32)
            owner = jnp.zeros(shape, jnp.int32)
            for m in range(batch):
                inside = (idx >= m * cap) & (idx < (m + 1) * cap)
                slot = idx - m * cap
                live = jnp.where(inside & (slot < counts[m]), 1.0, live)
                next_live = jnp.where(inside & (slot + 1 < counts[m]), 1.0, next_live)
                owner = jnp.where(inside, m, owner)
            return live, next_live, owner

        live_i, _, owner_i = per_slot(i)
        live_j, next_live_j, owner_j = per_slot(j)
        ep_j = jnp.broadcast_to(episode[...].astype(jnp.float32), shape)
        ep_i = jnp.broadcast_to(
            jnp.sum(jnp.where(i == j, ep_j, 0.0), axis=1, keepdims=True), shape
        )
        keep = (j >= i) & (ep_i == ep_j) & (owner_i == owner_j)
        w_buf[...] = jnp.where(keep, live_i * live_j, 0.0)
        ep_next = jnp.broadcast_to(
            jnp.sum(jnp.where(i == j + 1, ep_i, 0.0), axis=0, keepdims=True), shape
        )
        follow = jnp.where(ep_next == ep_j, next_live_j, 0.0)
        aux[0:8, :] = live_j[0:8]
        aux[8:16, :] = follow[0:8]

    def exchange_start(buf, send, recv, rs, c):
        for t in peers:
            pltpu.make_async_remote_copy(
                src_ref=buf.at[me, rs],
                dst_ref=buf.at[me, rs],
                send_sem=send.at[c, t],
                recv_sem=recv.at[c, me],
                device_id=to_peer(t),
                device_id_type=MESH,
            ).start()

    def exchange_wait(buf, send, recv, rs, c):
        for t in peers:
            pltpu.make_async_remote_copy(
                src_ref=buf.at[t, rs],
                dst_ref=buf.at[t, rs],
                send_sem=send.at[c, t],
                recv_sem=recv.at[c, t],
                device_id=to_peer(t),
                device_id_type=MESH,
            ).wait_recv()

    def exchange_done(buf, send, recv, rs, c):
        for t in peers:
            pltpu.make_async_remote_copy(
                src_ref=buf.at[me, rs],
                dst_ref=buf.at[me, rs],
                send_sem=send.at[c, t],
                recv_sem=recv.at[c, me],
                device_id=to_peer(t),
                device_id_type=MESH,
            ).wait_send()

    def total_of(buf, rs):
        total = buf[0, rs]
        for t in range(1, n_tp):
            total += buf[t, rs]
        return total

    def rows_of(c):
        return pl.ds(pl.multiple_of(c * CHUNK, CHUNK), CHUNK)

    def cols_of(s):
        return pl.ds(s * piece, piece)

    def forward_copy(c, s, target):
        return pltpu.make_async_remote_copy(
            src_ref=o_buf.at[rows_of(c), cols_of(s)],
            dst_ref=h_buf.at[rows_of(c), cols_of(s)],
            send_sem=f_send.at[c, s],
            recv_sem=f_recv.at[c, s],
            device_id=to_pipe(target),
            device_id_type=MESH,
        )

    def backward_copy(c, s, target):
        return pltpu.make_async_remote_copy(
            src_ref=q_buf.at[rows_of(c), cols_of(s)],
            dst_ref=g_buf.at[rows_of(c), cols_of(s)],
            send_sem=b_send.at[c, s],
            recv_sem=b_recv.at[c, s],
            device_id=to_pipe(target),
            device_id_type=MESH,
        )

    def forward(c, carry):
        rs = rows_of(c)
        total = jnp.zeros((CHUNK, inner), jnp.float32)
        for s in range(PIECES):

            @pl.when(p > 0)
            def _():
                forward_copy(c, s, p - 1).wait_recv()

            total += jnp.dot(
                h_buf[rs, cols_of(s)], down[cols_of(s), :], preferred_element_type=jnp.float32
            )
        fx[me, rs] = total
        exchange_start(fx, fx_send, fx_recv, rs, c)
        exchange_wait(fx, fx_send, fx_recv, rs, c)
        pre = total_of(fx, rs)
        act = jax.nn.silu(pre).astype(jnp.bfloat16)
        for s in range(PIECES):
            out = h_buf[rs, cols_of(s)].astype(jnp.float32) + jnp.dot(
                act, up[:, cols_of(s)], preferred_element_type=jnp.float32
            )
            o_buf[rs, cols_of(s)] = out.astype(jnp.bfloat16)

            @pl.when(p < last)
            def _():
                forward_copy(c, s, p + 1).start()

        pre_buf[rs] = pre
        act_buf[rs] = act

        @pl.when(is_last)
        def _():
            value = jnp.zeros((CHUNK, 1), jnp.float32)
            for s in range(PIECES):
                value += jnp.sum(
                    o_buf[rs, cols_of(s)].astype(jnp.float32)
                    * head[:, cols_of(s)].astype(jnp.float32),
                    axis=1,
                    keepdims=True,
                )
            vx[me, rs] = jnp.broadcast_to(value, (CHUNK, vx.shape[2]))

        return carry

    lax.fori_loop(0, chunks, forward, 0)

    every = pl.ds(0, rows)
    copies = [
        pltpu.make_async_copy(h_buf, h_out, local_sem.at[0]),
        pltpu.make_async_copy(act_buf, act_out, local_sem.at[1]),
    ]
    for copy in copies:
        copy.start()

    @pl.when(is_last)
    def _():
        exchange_start(vx, vx_send, vx_recv, every, 0)
        exchange_wait(vx, vx_send, vx_recv, every, 0)
        shape = (rows, rows)
        i = lax.broadcasted_iota(jnp.int32, shape, 0)
        j = lax.broadcasted_iota(jnp.int32, shape, 1)
        value = jnp.broadcast_to(total_of(vx, every)[:, 0:1], shape)
        value_row = jnp.sum(jnp.where(i == j, value, 0.0), axis=0, keepdims=True)
        next_row = jnp.sum(jnp.where(i == j + 1, value, 0.0), axis=0, keepdims=True)
        delta = (rewards[...] + aux[8:9, :] * next_row - value_row) * aux[0:1, :]
        adv = jnp.sum(w_buf[...] * delta, axis=1, keepdims=True)
        adv_all = jnp.broadcast_to(adv, shape)
        w_buf[...] = adv_all
        aux[0:8, :] = jnp.broadcast_to(
            jnp.sum(jnp.where(i == j, adv_all, 0.0), axis=0, keepdims=True), (8, rows)
        )
        for s in range(PIECES):
            g_buf[:, cols_of(s)] = (-adv * head[:, cols_of(s)].astype(jnp.float32)).astype(
                jnp.bfloat16
            )

    def backward(c, carry):
        rs = rows_of(c)
        total = jnp.zeros((CHUNK, inner), jnp.float32)
        for s in range(PIECES):

            @pl.when(p < last)
            def _():
                backward_copy(c, s, p + 1).wait_recv()

            total += lax.dot_general(
                g_buf[rs, cols_of(s)], up[:, cols_of(s)], NT, preferred_element_type=jnp.float32
            )
        bx[me, rs] = total
        exchange_start(bx, bx_send, bx_recv, rs, c)
        slope = derivative(pre_buf[rs])
        exchange_wait(bx, bx_send, bx_recv, rs, c)
        pg = (total_of(bx, rs) * slope).astype(jnp.bfloat16)

        @pl.when(p > 0)
        def _():
            for s in range(PIECES):
                out = g_buf[rs, cols_of(s)].astype(jnp.float32) + lax.dot_general(
                    pg, down[cols_of(s), :], NT, preferred_element_type=jnp.float32
                )
                q_buf[rs, cols_of(s)] = out.astype(jnp.bfloat16)
                backward_copy(c, s, p - 1).start()

        pg_buf[rs] = pg
        return carry

    lax.fori_loop(0, chunks, backward, 0)

    ends = [
        pltpu.make_async_copy(g_buf, g_out, local_sem.at[2]),
        pltpu.make_async_copy(pg_buf, pg_out, local_sem.at[3]),
    ]
    for copy in ends:
        copy.start()

    slice_width = width // n_pipe

    def message_copy(q):
        return pltpu.make_async_remote_copy(
            src_ref=msg.at[q],
            dst_ref=msg_in,
            send_sem=msg_send.at[q],
            recv_sem=msg_recv.at[0],
            device_id=to_pipe(q),
            device_id_type=MESH,
        )

    @pl.when(is_last)
    def _():
        adv_row = aux[0:1, :]
        adv = w_buf[:, 0:1]
        for b in range(width // block):
            cs = pl.ds(b * block, block)
            head_grad = jnp.sum(o_buf[:, cs].astype(jnp.float32) * -adv, axis=0, keepdims=True)
            for q in range(n_pipe):
                if q * slice_width // block == b:
                    msg[q, 0:1, :] = head_grad
                    msg[q, 1:2, 0:rows] = adv_row
        for q in range(last):
            message_copy(q).start()
        msg_out[...] = msg[last]

    @pl.when(p < last)
    def _():
        message_copy(last).wait_recv()
        msg_out[...] = msg_in[...]

    def finish(c, carry):
        rs = rows_of(c)
        for s in range(PIECES):

            @pl.when(p < last)
            def _():
                forward_copy(c, s, p + 1).wait_send()

            @pl.when(p > 0)
            def _():
                backward_copy(c, s, p - 1).wait_send()

        exchange_done(fx, fx_send, fx_recv, rs, c)
        exchange_done(bx, bx_send, bx_recv, rs, c)
        return carry

    lax.fori_loop(0, chunks, finish, 0)

    @pl.when(is_last)
    def _():
        exchange_done(vx, vx_send, vx_recv, every, 0)
        for q in range(last):
            message_copy(q).wait_send()

    for copy in copies + ends:
        copy.wait()


def local(hidden, rewards, counts, episode, down_weight, up_weight, head_weight):
    n_pipe = lax.axis_size("pipe")
    n_tp = lax.axis_size("tp")
    batch, cap, width = hidden.shape
    rows = batch * cap
    down, up = down_weight[0], up_weight[0]
    inner = down.shape[1]
    chunks = rows // CHUNK
    slice_width = width // n_pipe
    block = max(slice_width, 128)
    bf16, f32 = jnp.bfloat16, jnp.float32
    vmem = pl.BlockSpec(memory_space=pltpu.VMEM)
    smem = pl.BlockSpec(memory_space=pltpu.SMEM)
    anywhere = pl.BlockSpec(memory_space=pl.ANY)
    dma = pltpu.SemaphoreType.DMA
    h, act, pg, g, msg = pl.pallas_call(
        functools.partial(kernel, n_pipe, n_tp, batch),
        out_shape=(
            jax.ShapeDtypeStruct((rows, width), bf16),
            jax.ShapeDtypeStruct((rows, inner), bf16),
            jax.ShapeDtypeStruct((rows, inner), bf16),
            jax.ShapeDtypeStruct((rows, width), bf16),
            jax.ShapeDtypeStruct((8, block), f32),
        ),
        in_specs=[anywhere, vmem, smem, vmem, vmem, vmem, vmem],
        out_specs=(anywhere, anywhere, anywhere, anywhere, vmem),
        scratch_shapes=[
            pltpu.VMEM((rows, width), bf16),
            pltpu.VMEM((rows, width), bf16),
            pltpu.VMEM((rows, width), bf16),
            pltpu.VMEM((rows, width), bf16),
            pltpu.VMEM((rows, inner), bf16),
            pltpu.VMEM((rows, inner), bf16),
            pltpu.VMEM((rows, inner), f32),
            pltpu.VMEM((n_tp, rows, inner), f32),
            pltpu.VMEM((n_tp, rows, inner), f32),
            pltpu.VMEM((n_tp, rows, 128), f32),
            pltpu.VMEM((rows, rows), f32),
            pltpu.VMEM((16, rows), f32),
            pltpu.VMEM((n_pipe, 8, block), f32),
            pltpu.VMEM((8, block), f32),
            dma((chunks, PIECES)),
            dma((chunks, PIECES)),
            dma((chunks, PIECES)),
            dma((chunks, PIECES)),
            dma((chunks, n_tp)),
            dma((chunks, n_tp)),
            dma((chunks, n_tp)),
            dma((chunks, n_tp)),
            dma((1, n_tp)),
            dma((1, n_tp)),
            dma((n_pipe,)),
            dma((1,)),
            dma((4,)),
        ],
        compiler_params=pltpu.CompilerParams(
            collective_id=0, has_side_effects=True, vmem_limit_bytes=40 * 1024 * 1024
        ),
        name="adapters",
    )(
        hidden.reshape(rows, width),
        rewards.reshape(1, rows),
        counts,
        episode.reshape(1, rows),
        down,
        up,
        head_weight.reshape(1, width),
    )
    grad_down = jnp.einsum("nd,nk->dk", h, pg, preferred_element_type=f32)
    grad_up = jnp.einsum("nk,nd->kd", act, g, preferred_element_type=f32)
    offset = lax.rem(lax.axis_index("pipe") * slice_width, block)
    grad_head = lax.dynamic_slice(msg, (0, offset), (1, slice_width))
    advantages = msg[1, :rows].reshape(batch, cap)
    return (grad_down[None], grad_up[None], grad_head[None].reshape(1, slice_width), advantages)


def solution(mesh):
    return jax.shard_map(
        local,
        mesh=mesh,
        in_specs=(
            P(None, None, "tp"),
            P(),
            P(),
            P(),
            P("pipe", "tp", None),
            P("pipe", None, "tp"),
            P("tp"),
        ),
        out_specs=(P("pipe", "tp", None), P("pipe", None, "tp"), P("tp", "pipe"), P()),
        check_vma=False,
    )
```

```python
import functools

import jax
import jax.numpy as jnp
from jax import lax
from jax.experimental import pallas as pl
from jax.experimental.pallas import tpu as pltpu
from jax.sharding import PartitionSpec as P

MESH = pl.DeviceIdType.MESH
CHUNK = 8
PIECES = 4


def derivative(pre_act):
    s = jax.nn.sigmoid(pre_act)
    return s * (1.0 + pre_act * (1.0 - s))


def kernel(
    n_pipe,
    n_tp,
    batch,
    hidden,
    rewards,
    counts,
    episode,
    down,
    up,
    head,
    h_out,
    act_out,
    pg_out,
    g_out,
    msg_out,
    hid,
    h_buf,
    o_buf,
    g_buf,
    q_buf,
    flat,
    narrow,
    act_buf,
    pg_buf,
    pre_buf,
    wd,
    wu,
    wd_t,
    wu_t,
    hd,
    o_sum,
    ghx,
    vx,
    w_buf,
    aux,
    msg,
    msg_in,
    f_send,
    f_recv,
    b_send,
    b_recv,
    gx_send,
    gx_recv,
    px_send,
    px_recv,
    x_send,
    x_recv,
    msg_send,
    msg_recv,
    local_sem,
):
    p = lax.axis_index("pipe")
    me = lax.axis_index("tp")
    last = n_pipe - 1
    is_last = p == last
    width = h_buf.shape[1]
    rows = vx.shape[0]
    inner = wd.shape[2]
    own = rows // n_tp
    chunks = own // CHUNK
    fold = CHUNK * n_tp
    piece = width // PIECES
    peers = [lax.rem(me + i, n_tp) for i in range(1, n_tp)]
    block = msg.shape[2]
    sent = hid.shape[1]
    bf16, f32 = jnp.bfloat16, jnp.float32

    def to_pipe(q):
        return {"pipe": q, "tp": me}

    def to_peer(t):
        return {"pipe": p, "tp": t}

    barrier = pltpu.get_barrier_semaphore()
    for t in peers:
        pl.semaphore_signal(barrier, inc=1, device_id=to_peer(t), device_id_type=MESH)

    @pl.when(p > 0)
    def _():
        pl.semaphore_signal(barrier, inc=1, device_id=to_pipe(p - 1), device_id_type=MESH)

    @pl.when(p < last)
    def _():
        pl.semaphore_signal(barrier, inc=1, device_id=to_pipe(p + 1), device_id_type=MESH)
        pl.semaphore_signal(barrier, inc=1, device_id=to_pipe(last), device_id_type=MESH)

    @pl.when(is_last)
    def _():
        def greet(q, carry):
            pl.semaphore_signal(barrier, inc=1, device_id=to_pipe(q), device_id_type=MESH)
            return carry

        lax.fori_loop(0, last, greet, 0)

    @pl.when(p == 0)
    def _():
        pl.semaphore_wait(barrier, n_tp + 1)

    @pl.when((p > 0) & (p < last))
    def _():
        pl.semaphore_wait(barrier, n_tp + 2)

    @pl.when(is_last)
    def _():
        pl.semaphore_wait(barrier, n_tp + last)

    def peer_copy(src, dst, kind, t, slot):
        return pltpu.make_async_remote_copy(
            src_ref=src,
            dst_ref=dst,
            send_sem=x_send.at[kind, t],
            recv_sem=x_recv.at[kind, slot],
            device_id=to_peer(t),
            device_id_type=MESH,
        )

    def head_copy(t, slot):
        rs = pl.ds(pl.multiple_of(slot * CHUNK, CHUNK), CHUNK)
        return peer_copy(hd.at[rs], hd.at[rs], 6, t, slot)

    def from_row(t):
        return pl.multiple_of(t * own, own) if sent == own else 0

    def hidden_copy(t, slot):
        return peer_copy(hidden.at[pl.ds(from_row(t), sent)], hid.at[slot], 0, t, slot)

    loads = [
        pltpu.make_async_copy(down, wd.at[me], local_sem.at[0]),
        pltpu.make_async_copy(up, wu.at[me], local_sem.at[1]),
    ]
    own_hidden = pltpu.make_async_copy(
        hidden.at[pl.ds(from_row(me), sent)], hid.at[me], local_sem.at[2]
    )

    @pl.when(p == 0)
    def _():
        own_hidden.start()
        for t in peers:
            hidden_copy(t, me).start()

    for t in peers:
        peer_copy(down, wd.at[me], 1, t, me).start()
    loads[0].start()
    for t in peers:
        peer_copy(up, wu.at[me], 2, t, me).start()
    loads[1].start()

    @pl.when(is_last)
    def _():
        hd[pl.ds(pl.multiple_of(me * CHUNK, CHUNK), CHUNK), :] = jnp.broadcast_to(
            head[...].astype(f32), (CHUNK, width)
        )
        for t in peers:
            head_copy(t, me).start()

    @pl.when(is_last)
    def _():
        shape = (rows, rows)
        i = lax.broadcasted_iota(jnp.int32, shape, 0)
        j = lax.broadcasted_iota(jnp.int32, shape, 1)
        cap = rows // batch

        def per_slot(idx):
            live = jnp.zeros(shape, jnp.float32)
            next_live = jnp.zeros(shape, jnp.float32)
            owner = jnp.zeros(shape, jnp.int32)
            for m in range(batch):
                inside = (idx >= m * cap) & (idx < (m + 1) * cap)
                slot = idx - m * cap
                live = jnp.where(inside & (slot < counts[m]), 1.0, live)
                next_live = jnp.where(inside & (slot + 1 < counts[m]), 1.0, next_live)
                owner = jnp.where(inside, m, owner)
            return live, next_live, owner

        live_i, _, owner_i = per_slot(i)
        live_j, next_live_j, owner_j = per_slot(j)
        ep_j = jnp.broadcast_to(episode[...].astype(jnp.float32), shape)
        ep_i = jnp.broadcast_to(
            jnp.sum(jnp.where(i == j, ep_j, 0.0), axis=1, keepdims=True), shape
        )
        keep = (j >= i) & (ep_i == ep_j) & (owner_i == owner_j)
        w_buf[...] = jnp.where(keep, live_i * live_j, 0.0)
        ep_next = jnp.broadcast_to(
            jnp.sum(jnp.where(i == j + 1, ep_i, 0.0), axis=0, keepdims=True), shape
        )
        follow = jnp.where(ep_next == ep_j, next_live_j, 0.0)
        aux[0:8, :] = live_j[0:8]
        aux[8:16, :] = follow[0:8]

    @pl.when(p == 0)
    def _():
        own_hidden.wait()
        for t in peers:
            hidden_copy(t, t).wait_recv()

    loads[0].wait()
    for t in peers:
        peer_copy(down, wd.at[t], 1, t, t).wait_recv()
    loads[1].wait()
    for t in peers:
        peer_copy(up, wu.at[t], 2, t, t).wait_recv()

    def turn():
        size = min(256, width)

        def one(b, carry):
            cs = pl.ds(pl.multiple_of(b * size, size), size)
            for f in range(n_tp):
                wd_t[f, :, cs] = wd[f, cs, :].T
                wu_t[f, cs, :] = wu[f, :, cs].T
            return carry

        lax.fori_loop(0, width // size, one, 0)

    @pl.when(p >= n_pipe // 2)
    def _():
        turn()

    def short_rows(c):
        return pl.ds(pl.multiple_of(c * CHUNK, CHUNK), CHUNK)

    def global_rows(c):
        return pl.ds(pl.multiple_of(me * own + c * CHUNK, CHUNK), CHUNK)

    def out_rows(c):
        return pl.ds(pl.multiple_of(c * fold, fold), fold)

    def fold_rows(t, c):
        return pl.ds(pl.multiple_of((t * chunks + c) * fold, fold), fold)

    def cols_of(s):
        return pl.ds(s * piece, piece)

    def forward_copy(c, s, target):
        return pltpu.make_async_remote_copy(
            src_ref=o_buf.at[out_rows(c), cols_of(s)],
            dst_ref=h_buf.at[fold_rows(me, c), cols_of(s)],
            send_sem=f_send.at[c, s],
            recv_sem=f_recv.at[c, s],
            device_id=to_pipe(target),
            device_id_type=MESH,
        )

    def backward_copy(c, s, target):
        return pltpu.make_async_remote_copy(
            src_ref=q_buf.at[out_rows(c), cols_of(s)],
            dst_ref=g_buf.at[fold_rows(me, c), cols_of(s)],
            send_sem=b_send.at[c, s],
            recv_sem=b_recv.at[c, s],
            device_id=to_pipe(target),
            device_id_type=MESH,
        )

    def grad_copy(t, c, slot):
        return pltpu.make_async_remote_copy(
            src_ref=g_buf.at[fold_rows(slot, c)],
            dst_ref=g_buf.at[fold_rows(slot, c)],
            send_sem=gx_send.at[c, t],
            recv_sem=gx_recv.at[c, slot],
            device_id=to_peer(t),
            device_id_type=MESH,
        )

    def pre_grad_copy(t, c, slot):
        rs = pl.ds(pl.multiple_of(slot * own + c * CHUNK, CHUNK), CHUNK)
        return pltpu.make_async_remote_copy(
            src_ref=pg_buf.at[rs],
            dst_ref=pg_buf.at[rs],
            send_sem=px_send.at[c, t],
            recv_sem=px_recv.at[c, slot],
            device_id=to_peer(t),
            device_id_type=MESH,
        )

    def contract(x, weight, s):
        total = jnp.zeros((CHUNK, inner), f32)
        for f in range(n_tp):
            part = jnp.dot(x, weight[f, cols_of(s), :], preferred_element_type=f32)
            total += part[f * CHUNK : (f + 1) * CHUNK]
        return total

    def expand(x, weight, s):
        return jnp.concatenate(
            [
                jnp.dot(x, weight[f, :, cols_of(s)], preferred_element_type=f32)
                for f in range(n_tp)
            ],
            axis=0,
        )

    def forward(c, carry):
        rs = fold_rows(me, c)

        @pl.when(p == 0)
        def _():
            first = c * CHUNK if sent == own else me * own + c * CHUNK
            pair = pl.ds(pl.multiple_of(first // 16 * 16, 16), 16)
            odd = lax.rem(first // CHUNK, 2) == 1
            for s in range(PIECES):
                parts = []
                for f in range(n_tp):
                    both = hid[f, pair, cols_of(s)].astype(f32)
                    parts.append(jnp.where(odd, both[CHUNK:], both[:CHUNK]))
                h_buf[rs, cols_of(s)] = jnp.concatenate(parts, axis=0).astype(bf16)

        pre = jnp.zeros((CHUNK, inner), f32)
        for s in range(PIECES):

            @pl.when(p > 0)
            def _():
                forward_copy(c, s, p - 1).wait_recv()

            pre += contract(h_buf[rs, cols_of(s)], wd, s)
        act = jax.nn.silu(pre).astype(bf16)
        for s in range(PIECES):
            out = h_buf[rs, cols_of(s)].astype(f32) + expand(act, wu, s)
            o_buf[out_rows(c), cols_of(s)] = out.astype(bf16)

            @pl.when(p < last)
            def _():
                forward_copy(c, s, p + 1).start()

        pre_buf[short_rows(c)] = pre
        act_buf[global_rows(c)] = act.astype(f32)

        @pl.when(is_last)
        def _():
            value = jnp.zeros((fold, 1), f32)
            for s in range(PIECES):
                value += jnp.sum(
                    o_buf[out_rows(c), cols_of(s)].astype(f32) * hd[:, cols_of(s)],
                    axis=1,
                    keepdims=True,
                )
            total = value[0:CHUNK]
            for f in range(1, n_tp):
                total += value[f * CHUNK : (f + 1) * CHUNK]
            vx[global_rows(c)] = jnp.broadcast_to(total, (CHUNK, vx.shape[1]))

        return carry

    @pl.when(is_last)
    def _():
        for t in peers:
            head_copy(t, t).wait_recv()

    lax.fori_loop(0, chunks, forward, 0)

    def own_rows(t):
        return pl.ds(pl.multiple_of(t * own, own), own)

    def kept_copy(t, slot):
        rs = pl.ds(pl.multiple_of(slot * chunks * fold, chunks * fold), chunks * fold)
        return peer_copy(h_buf.at[rs], h_buf.at[rs], 3, t, slot)

    def act_copy(t, slot):
        return peer_copy(act_buf.at[own_rows(slot)], act_buf.at[own_rows(slot)], 4, t, slot)

    def value_copy(t, slot):
        return peer_copy(vx.at[own_rows(slot)], vx.at[own_rows(slot)], 5, t, slot)

    @pl.when(is_last)
    def _():
        for t in peers:
            value_copy(t, me).start()
        for t in peers:
            value_copy(t, t).wait_recv()
        shape = (rows, rows)
        i = lax.broadcasted_iota(jnp.int32, shape, 0)
        j = lax.broadcasted_iota(jnp.int32, shape, 1)
        value = jnp.broadcast_to(vx[:, 0:1], shape)
        value_row = jnp.sum(jnp.where(i == j, value, 0.0), axis=0, keepdims=True)
        next_row = jnp.sum(jnp.where(i == j + 1, value, 0.0), axis=0, keepdims=True)
        delta = (rewards[...] + aux[8:9, :] * next_row - value_row) * aux[0:1, :]
        adv = jnp.sum(w_buf[...] * delta, axis=1, keepdims=True)
        adv_all = jnp.broadcast_to(adv, shape)
        w_buf[...] = adv_all
        aux[0:8, :] = jnp.broadcast_to(
            jnp.sum(jnp.where(i == j, adv_all, 0.0), axis=0, keepdims=True), (8, rows)
        )

    for t in peers:
        kept_copy(t, me).start()
        act_copy(t, me).start()

    @pl.when(p < n_pipe // 2)
    def _():
        turn()

    def signed_grad(c):
        grad = -w_buf[global_rows(c), 0:1]
        return jnp.concatenate([grad] * n_tp, axis=0)

    def backward(c, carry):
        rs = fold_rows(me, c)

        @pl.when(is_last)
        def _():
            grad = signed_grad(c)
            for s in range(PIECES):
                g_buf[rs, cols_of(s)] = (grad * hd[:, cols_of(s)]).astype(bf16)

        total = jnp.zeros((CHUNK, inner), f32)
        for s in range(PIECES):

            @pl.when(p < last)
            def _():
                backward_copy(c, s, p + 1).wait_recv()

            total += contract(g_buf[rs, cols_of(s)], wu_t, s)
        pg = (total * derivative(pre_buf[short_rows(c)])).astype(bf16)

        @pl.when(p > 0)
        def _():
            for s in range(PIECES):
                out = g_buf[rs, cols_of(s)].astype(f32) + expand(pg, wd_t, s)
                q_buf[out_rows(c), cols_of(s)] = out.astype(bf16)
                backward_copy(c, s, p - 1).start()

        pg_buf[global_rows(c)] = pg.astype(f32)
        for t in peers:
            grad_copy(t, c, me).start()
            pre_grad_copy(t, c, me).start()
        return carry

    def unfold(buf, k):
        parts = []
        for half in range(2):
            start = pl.multiple_of((2 * k + half) * fold, fold)
            both = buf[pl.ds(start, fold)].astype(f32)
            mine = both[0:CHUNK]
            for f in range(1, n_tp):
                mine = jnp.where(me == f, both[f * CHUNK : (f + 1) * CHUNK], mine)
            parts.append(mine)
        return jnp.concatenate(parts, axis=0).astype(bf16)

    def flat_pass(buf, index):
        def one(k, carry):
            flat[index, pl.ds(pl.multiple_of(k * 16, 16), 16)] = unfold(buf, k)
            return carry

        lax.fori_loop(0, rows // 16, one, 0)

    def keep():
        for t in peers:
            kept_copy(t, t).wait_recv()
            act_copy(t, t).wait_recv()
        flat_pass(h_buf, 0)
        narrow[0] = act_buf[...].astype(bf16)
        copies[0].start()
        copies[1].start()

    copies = [
        pltpu.make_async_copy(flat.at[0], h_out, local_sem.at[0]),
        pltpu.make_async_copy(narrow.at[0], act_out, local_sem.at[1]),
        pltpu.make_async_copy(flat.at[1], g_out, local_sem.at[2]),
        pltpu.make_async_copy(narrow.at[1], pg_out, local_sem.at[3]),
    ]

    @pl.when(p < last)
    def _():
        keep()

    lax.fori_loop(0, chunks, backward, 0)

    @pl.when(is_last)
    def _():
        keep()

    def gather(c, carry):
        for t in peers:
            grad_copy(t, c, t).wait_recv()
            pre_grad_copy(t, c, t).wait_recv()
        return carry

    lax.fori_loop(0, chunks, gather, 0)
    flat_pass(g_buf, 1)
    narrow[1] = pg_buf[...].astype(bf16)
    copies[2].start()
    copies[3].start()

    slice_width = width // n_pipe

    def message_copy(q):
        return pltpu.make_async_remote_copy(
            src_ref=msg.at[q],
            dst_ref=msg_in,
            send_sem=msg_send.at[q],
            recv_sem=msg_recv.at[0],
            device_id=to_pipe(q),
            device_id_type=MESH,
        )

    def head_rows(t):
        return pl.ds(pl.multiple_of(t * CHUNK, CHUNK), CHUNK)

    def head_grad_copy(t, slot):
        return peer_copy(o_sum.at[head_rows(t)], ghx.at[slot], 7, t, slot)

    @pl.when(is_last)
    def _():
        for s in range(PIECES):
            acc = jnp.zeros((fold, piece), f32)
            for c in range(chunks):
                acc += o_buf[out_rows(c), cols_of(s)].astype(f32) * signed_grad(c)
            o_sum[:, cols_of(s)] = acc
        ghx[me] = o_sum[head_rows(me)]
        for t in peers:
            head_grad_copy(t, me).start()
        for t in peers:
            head_grad_copy(t, t).wait_recv()
        adv_row = aux[0:1, :]
        for b in range(width // block):
            cs = pl.ds(b * block, block)
            acc = ghx[0, :, cs]
            for t in range(1, n_tp):
                acc += ghx[t, :, cs]
            head_grad = jnp.sum(acc, axis=0, keepdims=True)
            for q in range(n_pipe):
                if q * slice_width // block == b:
                    msg[q, 0:1, :] = head_grad
                    msg[q, 1:2, 0:rows] = adv_row
        for q in range(last):
            message_copy(q).start()
        msg_out[...] = msg[last]

    @pl.when(p < last)
    def _():
        message_copy(last).wait_recv()
        msg_out[...] = msg_in[...]

    def finish(c, carry):
        for s in range(PIECES):

            @pl.when(p < last)
            def _():
                forward_copy(c, s, p + 1).wait_send()

            @pl.when(p > 0)
            def _():
                backward_copy(c, s, p - 1).wait_send()

        for t in peers:
            grad_copy(t, c, me).wait_send()
            pre_grad_copy(t, c, me).wait_send()
        return carry

    lax.fori_loop(0, chunks, finish, 0)

    @pl.when(p == 0)
    def _():
        for t in peers:
            hidden_copy(t, me).wait_send()

    for t in peers:
        peer_copy(down, wd.at[me], 1, t, me).wait_send()
        peer_copy(up, wu.at[me], 2, t, me).wait_send()
        kept_copy(t, me).wait_send()
        act_copy(t, me).wait_send()

    @pl.when(is_last)
    def _():
        for t in peers:
            head_copy(t, me).wait_send()
            value_copy(t, me).wait_send()
            head_grad_copy(t, me).wait_send()
        for q in range(last):
            message_copy(q).wait_send()

    for copy in copies:
        copy.wait()


def local(hidden, rewards, counts, episode, down_weight, up_weight, head_weight):
    n_pipe = lax.axis_size("pipe")
    n_tp = lax.axis_size("tp")
    batch, cap, width = hidden.shape
    rows = batch * cap
    down, up = down_weight[0], up_weight[0]
    inner = down.shape[1]
    own = rows // n_tp
    sent = own if own % 16 == 0 else rows
    chunks = own // CHUNK
    slice_width = width // n_pipe
    block = max(slice_width, 128)
    bf16, f32 = jnp.bfloat16, jnp.float32
    vmem = pl.BlockSpec(memory_space=pltpu.VMEM)
    smem = pl.BlockSpec(memory_space=pltpu.SMEM)
    anywhere = pl.BlockSpec(memory_space=pl.ANY)
    dma = pltpu.SemaphoreType.DMA
    h, act, pg, g, msg = pl.pallas_call(
        functools.partial(kernel, n_pipe, n_tp, batch),
        out_shape=(
            jax.ShapeDtypeStruct((rows, width), bf16),
            jax.ShapeDtypeStruct((rows, inner), bf16),
            jax.ShapeDtypeStruct((rows, inner), bf16),
            jax.ShapeDtypeStruct((rows, width), bf16),
            jax.ShapeDtypeStruct((8, block), f32),
        ),
        in_specs=[anywhere, vmem, smem, vmem, anywhere, anywhere, vmem],
        out_specs=(anywhere, anywhere, anywhere, anywhere, vmem),
        scratch_shapes=[
            pltpu.VMEM((n_tp, sent, width), bf16),
            pltpu.VMEM((n_tp * rows, width), bf16),
            pltpu.VMEM((rows, width), bf16),
            pltpu.VMEM((n_tp * rows, width), bf16),
            pltpu.VMEM((rows, width), bf16),
            pltpu.VMEM((2, rows, width), bf16),
            pltpu.VMEM((2, rows, inner), bf16),
            pltpu.VMEM((rows, inner), f32),
            pltpu.VMEM((rows, inner), f32),
            pltpu.VMEM((own, inner), f32),
            pltpu.VMEM((n_tp, width, inner), bf16),
            pltpu.VMEM((n_tp, inner, width), bf16),
            pltpu.VMEM((n_tp, inner, width), bf16),
            pltpu.VMEM((n_tp, width, inner), bf16),
            pltpu.VMEM((n_tp * CHUNK, width), f32),
            pltpu.VMEM((n_tp * CHUNK, width), f32),
            pltpu.VMEM((n_tp, CHUNK, width), f32),
            pltpu.VMEM((rows, 128), f32),
            pltpu.VMEM((rows, rows), f32),
            pltpu.VMEM((16, rows), f32),
            pltpu.VMEM((n_pipe, 8, block), f32),
            pltpu.VMEM((8, block), f32),
            dma((chunks, PIECES)),
            dma((chunks, PIECES)),
            dma((chunks, PIECES)),
            dma((chunks, PIECES)),
            dma((chunks, n_tp)),
            dma((chunks, n_tp)),
            dma((chunks, n_tp)),
            dma((chunks, n_tp)),
            dma((8, n_tp)),
            dma((8, n_tp)),
            dma((n_pipe,)),
            dma((1,)),
            dma((4,)),
        ],
        compiler_params=pltpu.CompilerParams(
            collective_id=0, has_side_effects=True, vmem_limit_bytes=56 * 1024 * 1024
        ),
        name="adapters",
    )(
        hidden.reshape(rows, width),
        rewards.reshape(1, rows),
        counts,
        episode.reshape(1, rows),
        down,
        up,
        head_weight.reshape(1, width),
    )
    grad_down = jnp.einsum("nd,nk->dk", h, pg, preferred_element_type=f32)
    grad_up = jnp.einsum("nk,nd->kd", act, g, preferred_element_type=f32)
    offset = lax.rem(lax.axis_index("pipe") * slice_width, block)
    grad_head = lax.dynamic_slice(msg, (0, offset), (1, slice_width))
    advantages = msg[1, :rows].reshape(batch, cap)
    return (grad_down[None], grad_up[None], grad_head[None].reshape(1, slice_width), advantages)


def solution(mesh):
    return jax.shard_map(
        local,
        mesh=mesh,
        in_specs=(
            P(None, None, "tp"),
            P(),
            P(),
            P(),
            P("pipe", "tp", None),
            P("pipe", None, "tp"),
            P("tp"),
        ),
        out_specs=(P("pipe", "tp", None), P("pipe", None, "tp"), P("tp", "pipe"), P()),
        check_vma=False,
    )
```

```python
import functools

import jax
import jax.numpy as jnp
from jax import lax
from jax.experimental import pallas as pl
from jax.experimental.pallas import tpu as pltpu
from jax.sharding import PartitionSpec as P

MESH = pl.DeviceIdType.MESH
CHUNK = 8
PIECES = 4


def derivative(pre_act):
    s = jax.nn.sigmoid(pre_act)
    return s * (1.0 + pre_act * (1.0 - s))


def kernel(
    n_pipe,
    n_tp,
    batch,
    hidden,
    rewards,
    counts,
    episode,
    down,
    up,
    head,
    h_out,
    act_out,
    pg_out,
    g_out,
    msg_out,
    hid,
    h_buf,
    o_buf,
    g_buf,
    q_buf,
    flat,
    narrow,
    act_buf,
    pg_buf,
    pre_buf,
    wd,
    wu,
    wd_t,
    wu_t,
    hd,
    o_sum,
    ghx,
    vx,
    w_buf,
    aux,
    msg,
    msg_in,
    f_send,
    f_recv,
    b_send,
    b_recv,
    gx_send,
    gx_recv,
    px_send,
    px_recv,
    x_send,
    x_recv,
    msg_send,
    msg_recv,
    local_sem,
):
    p = lax.axis_index("pipe")
    me = lax.axis_index("tp")
    last = n_pipe - 1
    is_last = p == last
    width = h_buf.shape[1]
    rows = vx.shape[0]
    inner = wd.shape[2]
    own = rows // n_tp
    chunks = own // CHUNK
    fold = CHUNK * n_tp
    piece = width // PIECES
    peers = [lax.rem(me + i, n_tp) for i in range(1, n_tp)]
    block = msg.shape[2]
    sent = hid.shape[1]
    bf16, f32 = jnp.bfloat16, jnp.float32

    def to_pipe(q):
        return {"pipe": q, "tp": me}

    def to_peer(t):
        return {"pipe": p, "tp": t}

    barrier = pltpu.get_barrier_semaphore()
    for t in peers:
        pl.semaphore_signal(barrier, inc=1, device_id=to_peer(t), device_id_type=MESH)

    @pl.when(p > 0)
    def _():
        pl.semaphore_signal(barrier, inc=1, device_id=to_pipe(p - 1), device_id_type=MESH)

    @pl.when(p < last)
    def _():
        pl.semaphore_signal(barrier, inc=1, device_id=to_pipe(p + 1), device_id_type=MESH)
        pl.semaphore_signal(barrier, inc=1, device_id=to_pipe(last), device_id_type=MESH)

    @pl.when(is_last)
    def _():
        def greet(q, carry):
            pl.semaphore_signal(barrier, inc=1, device_id=to_pipe(q), device_id_type=MESH)
            return carry

        lax.fori_loop(0, last, greet, 0)

    @pl.when(p == 0)
    def _():
        pl.semaphore_wait(barrier, n_tp + 1)

    @pl.when((p > 0) & (p < last))
    def _():
        pl.semaphore_wait(barrier, n_tp + 2)

    @pl.when(is_last)
    def _():
        pl.semaphore_wait(barrier, n_tp + last)

    def peer_copy(src, dst, kind, t, slot):
        return pltpu.make_async_remote_copy(
            src_ref=src,
            dst_ref=dst,
            send_sem=x_send.at[kind, t],
            recv_sem=x_recv.at[kind, slot],
            device_id=to_peer(t),
            device_id_type=MESH,
        )

    def head_copy(t, slot):
        rs = pl.ds(pl.multiple_of(slot * CHUNK, CHUNK), CHUNK)
        return peer_copy(hd.at[rs], hd.at[rs], 6, t, slot)

    def from_row(t):
        return pl.multiple_of(t * own, own) if sent == own else 0

    def hidden_copy(t, slot):
        return peer_copy(hidden.at[pl.ds(from_row(t), sent)], hid.at[slot], 0, t, slot)

    loads = [
        pltpu.make_async_copy(down, wd.at[me], local_sem.at[0]),
        pltpu.make_async_copy(up, wu.at[me], local_sem.at[1]),
    ]
    own_hidden = pltpu.make_async_copy(
        hidden.at[pl.ds(from_row(me), sent)], hid.at[me], local_sem.at[2]
    )

    @pl.when(p == 0)
    def _():
        own_hidden.start()
        for t in peers:
            hidden_copy(t, me).start()

    for t in peers:
        peer_copy(down, wd.at[me], 1, t, me).start()
    loads[0].start()
    for t in peers:
        peer_copy(up, wu.at[me], 2, t, me).start()
    loads[1].start()

    @pl.when(is_last)
    def _():
        hd[pl.ds(pl.multiple_of(me * CHUNK, CHUNK), CHUNK), :] = jnp.broadcast_to(
            head[...].astype(f32).reshape(1, width), (CHUNK, width)
        )
        for t in peers:
            head_copy(t, me).start()

    @pl.when(is_last)
    def _():
        shape = (rows, rows)
        i = lax.broadcasted_iota(jnp.int32, shape, 0)
        j = lax.broadcasted_iota(jnp.int32, shape, 1)
        cap = rows // batch
        for m in range(batch):
            aux[16:17, m * cap : (m + 1) * cap] = rewards[m : m + 1, :]
            aux[24:25, m * cap : (m + 1) * cap] = episode[m : m + 1, :].astype(f32)

        def per_slot(idx):
            live = jnp.zeros(shape, jnp.float32)
            next_live = jnp.zeros(shape, jnp.float32)
            owner = jnp.zeros(shape, jnp.int32)
            for m in range(batch):
                inside = (idx >= m * cap) & (idx < (m + 1) * cap)
                slot = idx - m * cap
                live = jnp.where(inside & (slot < counts[m]), 1.0, live)
                next_live = jnp.where(inside & (slot + 1 < counts[m]), 1.0, next_live)
                owner = jnp.where(inside, m, owner)
            return live, next_live, owner

        live_i, _, owner_i = per_slot(i)
        live_j, next_live_j, owner_j = per_slot(j)
        ep_j = jnp.broadcast_to(aux[24:25, :], shape)
        ep_i = jnp.broadcast_to(
            jnp.sum(jnp.where(i == j, ep_j, 0.0), axis=1, keepdims=True), shape
        )
        keep = (j >= i) & (ep_i == ep_j) & (owner_i == owner_j)
        w_buf[...] = jnp.where(keep, live_i * live_j, 0.0)
        ep_next = jnp.broadcast_to(
            jnp.sum(jnp.where(i == j + 1, ep_i, 0.0), axis=0, keepdims=True), shape
        )
        follow = jnp.where(ep_next == ep_j, next_live_j, 0.0)
        aux[0:8, :] = live_j[0:8]
        aux[8:16, :] = follow[0:8]

    @pl.when(p == 0)
    def _():
        own_hidden.wait()
        for t in peers:
            hidden_copy(t, t).wait_recv()

    loads[0].wait()
    for t in peers:
        peer_copy(down, wd.at[t], 1, t, t).wait_recv()
    loads[1].wait()
    for t in peers:
        peer_copy(up, wu.at[t], 2, t, t).wait_recv()

    def turn():
        size = min(256, width)

        def one(b, carry):
            cs = pl.ds(pl.multiple_of(b * size, size), size)
            for f in range(n_tp):
                wd_t[f, :, cs] = wd[f, cs, :].T
                wu_t[f, cs, :] = wu[f, :, cs].T
            return carry

        lax.fori_loop(0, width // size, one, 0)

    @pl.when(p >= n_pipe // 2)
    def _():
        turn()

    def short_rows(c):
        return pl.ds(pl.multiple_of(c * CHUNK, CHUNK), CHUNK)

    def global_rows(c):
        return pl.ds(pl.multiple_of(me * own + c * CHUNK, CHUNK), CHUNK)

    def out_rows(c):
        return pl.ds(pl.multiple_of(c * fold, fold), fold)

    def fold_rows(t, c):
        return pl.ds(pl.multiple_of((t * chunks + c) * fold, fold), fold)

    def cols_of(s):
        return pl.ds(s * piece, piece)

    def forward_copy(c, s, target):
        return pltpu.make_async_remote_copy(
            src_ref=o_buf.at[out_rows(c), cols_of(s)],
            dst_ref=h_buf.at[fold_rows(me, c), cols_of(s)],
            send_sem=f_send.at[c, s],
            recv_sem=f_recv.at[c, s],
            device_id=to_pipe(target),
            device_id_type=MESH,
        )

    def backward_copy(c, s, target):
        return pltpu.make_async_remote_copy(
            src_ref=q_buf.at[out_rows(c), cols_of(s)],
            dst_ref=g_buf.at[fold_rows(me, c), cols_of(s)],
            send_sem=b_send.at[c, s],
            recv_sem=b_recv.at[c, s],
            device_id=to_pipe(target),
            device_id_type=MESH,
        )

    def grad_copy(t, c, slot):
        return pltpu.make_async_remote_copy(
            src_ref=g_buf.at[fold_rows(slot, c)],
            dst_ref=g_buf.at[fold_rows(slot, c)],
            send_sem=gx_send.at[c, t],
            recv_sem=gx_recv.at[c, slot],
            device_id=to_peer(t),
            device_id_type=MESH,
        )

    def pre_grad_copy(t, c, slot):
        rs = pl.ds(pl.multiple_of(slot * own + c * CHUNK, CHUNK), CHUNK)
        return pltpu.make_async_remote_copy(
            src_ref=pg_buf.at[rs],
            dst_ref=pg_buf.at[rs],
            send_sem=px_send.at[c, t],
            recv_sem=px_recv.at[c, slot],
            device_id=to_peer(t),
            device_id_type=MESH,
        )

    def contract(x, weight, s):
        total = jnp.zeros((CHUNK, inner), f32)
        for f in range(n_tp):
            part = jnp.dot(x, weight[f, cols_of(s), :], preferred_element_type=f32)
            total += part[f * CHUNK : (f + 1) * CHUNK]
        return total

    def expand(x, weight, s):
        return jnp.concatenate(
            [
                jnp.dot(x, weight[f, :, cols_of(s)], preferred_element_type=f32)
                for f in range(n_tp)
            ],
            axis=0,
        )

    def forward(first_layer, final_layer, c, carry):
        rs = fold_rows(me, c)

        if first_layer:
            first = c * CHUNK if sent == own else me * own + c * CHUNK
            pair = pl.ds(pl.multiple_of(first // 16 * 16, 16), 16)
            odd = lax.rem(first // CHUNK, 2) == 1
            for s in range(PIECES):
                parts = []
                for f in range(n_tp):
                    both = hid[f, pair, cols_of(s)].astype(f32)
                    parts.append(jnp.where(odd, both[CHUNK:], both[:CHUNK]))
                h_buf[rs, cols_of(s)] = jnp.concatenate(parts, axis=0).astype(bf16)

        pre = jnp.zeros((CHUNK, inner), f32)
        for s in range(PIECES):

            if not first_layer:
                forward_copy(c, s, p - 1).wait_recv()

            pre += contract(h_buf[rs, cols_of(s)], wd, s)
        act = jax.nn.silu(pre).astype(bf16)
        for s in range(PIECES):
            out = h_buf[rs, cols_of(s)].astype(f32) + expand(act, wu, s)
            o_buf[out_rows(c), cols_of(s)] = out.astype(bf16)

            if not final_layer:
                forward_copy(c, s, p + 1).start()

        pre_buf[short_rows(c)] = pre
        act_buf[global_rows(c)] = act.astype(f32)

        if final_layer:
            value = jnp.zeros((fold, 1), f32)
            for s in range(PIECES):
                value += jnp.sum(
                    o_buf[out_rows(c), cols_of(s)].astype(f32) * hd[:, cols_of(s)],
                    axis=1,
                    keepdims=True,
                )
            total = value[0:CHUNK]
            for f in range(1, n_tp):
                total += value[f * CHUNK : (f + 1) * CHUNK]
            vx[global_rows(c)] = jnp.broadcast_to(total, (CHUNK, vx.shape[1]))

        return carry

    def by_place(body):
        @pl.when(p == 0)
        def _():
            lax.fori_loop(0, chunks, functools.partial(body, True, n_pipe == 1), 0)

        @pl.when((p > 0) & (p < last))
        def _():
            lax.fori_loop(0, chunks, functools.partial(body, False, False), 0)

        @pl.when((p > 0) & is_last)
        def _():
            lax.fori_loop(0, chunks, functools.partial(body, False, True), 0)

    @pl.when(is_last)
    def _():
        for t in peers:
            head_copy(t, t).wait_recv()

    by_place(forward)

    def own_rows(t):
        return pl.ds(pl.multiple_of(t * own, own), own)

    def kept_copy(t, slot):
        rs = pl.ds(pl.multiple_of(slot * chunks * fold, chunks * fold), chunks * fold)
        return peer_copy(h_buf.at[rs], h_buf.at[rs], 3, t, slot)

    def act_copy(t, slot):
        return peer_copy(act_buf.at[own_rows(slot)], act_buf.at[own_rows(slot)], 4, t, slot)

    def value_copy(t, slot):
        return peer_copy(vx.at[own_rows(slot)], vx.at[own_rows(slot)], 5, t, slot)

    @pl.when(is_last)
    def _():
        for t in peers:
            value_copy(t, me).start()
        for t in peers:
            value_copy(t, t).wait_recv()
        shape = (rows, rows)
        i = lax.broadcasted_iota(jnp.int32, shape, 0)
        j = lax.broadcasted_iota(jnp.int32, shape, 1)
        value = jnp.broadcast_to(vx[:, 0:1], shape)
        value_row = jnp.sum(jnp.where(i == j, value, 0.0), axis=0, keepdims=True)
        next_row = jnp.sum(jnp.where(i == j + 1, value, 0.0), axis=0, keepdims=True)
        delta = (aux[16:17, :] + aux[8:9, :] * next_row - value_row) * aux[0:1, :]
        adv = jnp.sum(w_buf[...] * delta, axis=1, keepdims=True)
        adv_all = jnp.broadcast_to(adv, shape)
        w_buf[...] = adv_all
        aux[0:8, :] = jnp.broadcast_to(
            jnp.sum(jnp.where(i == j, adv_all, 0.0), axis=0, keepdims=True), (8, rows)
        )

    for t in peers:
        kept_copy(t, me).start()
        act_copy(t, me).start()

    @pl.when(p < n_pipe // 2)
    def _():
        turn()

    def signed_grad(c):
        grad = -w_buf[global_rows(c), 0:1]
        return jnp.concatenate([grad] * n_tp, axis=0)

    def backward(first_layer, final_layer, c, carry):
        rs = fold_rows(me, c)

        if final_layer:
            grad = signed_grad(c)
            for s in range(PIECES):
                g_buf[rs, cols_of(s)] = (grad * hd[:, cols_of(s)]).astype(bf16)

        total = jnp.zeros((CHUNK, inner), f32)
        for s in range(PIECES):

            if not final_layer:
                backward_copy(c, s, p + 1).wait_recv()

            total += contract(g_buf[rs, cols_of(s)], wu_t, s)
        pg = (total * derivative(pre_buf[short_rows(c)])).astype(bf16)

        if not first_layer:
            for s in range(PIECES):
                out = g_buf[rs, cols_of(s)].astype(f32) + expand(pg, wd_t, s)
                q_buf[out_rows(c), cols_of(s)] = out.astype(bf16)
                backward_copy(c, s, p - 1).start()

        pg_buf[global_rows(c)] = pg.astype(f32)
        for t in peers:
            grad_copy(t, c, me).start()
            pre_grad_copy(t, c, me).start()
        return carry

    def unfold(buf, k):
        parts = []
        for half in range(2):
            start = pl.multiple_of((2 * k + half) * fold, fold)
            both = buf[pl.ds(start, fold)].astype(f32)
            mine = both[0:CHUNK]
            for f in range(1, n_tp):
                mine = jnp.where(me == f, both[f * CHUNK : (f + 1) * CHUNK], mine)
            parts.append(mine)
        return jnp.concatenate(parts, axis=0).astype(bf16)

    def flat_pass(buf, index):
        def one(k, carry):
            flat[index, pl.ds(pl.multiple_of(k * 16, 16), 16)] = unfold(buf, k)
            return carry

        lax.fori_loop(0, rows // 16, one, 0)

    def keep():
        for t in peers:
            kept_copy(t, t).wait_recv()
            act_copy(t, t).wait_recv()
        flat_pass(h_buf, 0)
        narrow[0] = act_buf[...].astype(bf16)
        copies[0].start()
        copies[1].start()

    copies = [
        pltpu.make_async_copy(flat.at[0], h_out, local_sem.at[0]),
        pltpu.make_async_copy(narrow.at[0], act_out, local_sem.at[1]),
        pltpu.make_async_copy(flat.at[1], g_out, local_sem.at[2]),
        pltpu.make_async_copy(narrow.at[1], pg_out, local_sem.at[3]),
    ]

    @pl.when(p < last)
    def _():
        keep()

    by_place(backward)

    @pl.when(is_last)
    def _():
        keep()

    def gather(c, carry):
        for t in peers:
            grad_copy(t, c, t).wait_recv()
            pre_grad_copy(t, c, t).wait_recv()
        return carry

    lax.fori_loop(0, chunks, gather, 0)
    flat_pass(g_buf, 1)
    narrow[1] = pg_buf[...].astype(bf16)
    copies[2].start()
    copies[3].start()

    slice_width = width // n_pipe

    def message_copy(q):
        return pltpu.make_async_remote_copy(
            src_ref=msg.at[q],
            dst_ref=msg_in,
            send_sem=msg_send.at[q],
            recv_sem=msg_recv.at[0],
            device_id=to_pipe(q),
            device_id_type=MESH,
        )

    def head_rows(t):
        return pl.ds(pl.multiple_of(t * CHUNK, CHUNK), CHUNK)

    def head_grad_copy(t, slot):
        return peer_copy(o_sum.at[head_rows(t)], ghx.at[slot], 7, t, slot)

    @pl.when(is_last)
    def _():
        for s in range(PIECES):
            acc = jnp.zeros((fold, piece), f32)
            for c in range(chunks):
                acc += o_buf[out_rows(c), cols_of(s)].astype(f32) * signed_grad(c)
            o_sum[:, cols_of(s)] = acc
        ghx[me] = o_sum[head_rows(me)]
        for t in peers:
            head_grad_copy(t, me).start()
        for t in peers:
            head_grad_copy(t, t).wait_recv()
        adv_row = aux[0:1, :]
        for b in range(width // block):
            cs = pl.ds(b * block, block)
            acc = ghx[0, :, cs]
            for t in range(1, n_tp):
                acc += ghx[t, :, cs]
            head_grad = jnp.sum(acc, axis=0, keepdims=True)
            for q in range(n_pipe):
                if q * slice_width // block == b:
                    msg[q, 0:1, :] = head_grad
                    msg[q, 1:2, 0:rows] = adv_row
        for q in range(last):
            message_copy(q).start()
        msg_out[...] = msg[last]

    @pl.when(p < last)
    def _():
        message_copy(last).wait_recv()
        msg_out[...] = msg_in[...]

    def finish(c, carry):
        for s in range(PIECES):

            @pl.when(p < last)
            def _():
                forward_copy(c, s, p + 1).wait_send()

            @pl.when(p > 0)
            def _():
                backward_copy(c, s, p - 1).wait_send()

        for t in peers:
            grad_copy(t, c, me).wait_send()
            pre_grad_copy(t, c, me).wait_send()
        return carry

    lax.fori_loop(0, chunks, finish, 0)

    @pl.when(p == 0)
    def _():
        for t in peers:
            hidden_copy(t, me).wait_send()

    for t in peers:
        peer_copy(down, wd.at[me], 1, t, me).wait_send()
        peer_copy(up, wu.at[me], 2, t, me).wait_send()
        kept_copy(t, me).wait_send()
        act_copy(t, me).wait_send()

    @pl.when(is_last)
    def _():
        for t in peers:
            head_copy(t, me).wait_send()
            value_copy(t, me).wait_send()
            head_grad_copy(t, me).wait_send()
        for q in range(last):
            message_copy(q).wait_send()

    for copy in copies:
        copy.wait()


def gradients(h, act, pg, g, msg, grad_down, grad_up, head_row, advantages):
    over_rows = (((0,), (0,)), ((), ()))
    grad_down[...] = lax.dot_general(
        h[...], pg[...], over_rows, preferred_element_type=jnp.float32
    )
    grad_up[...] = lax.dot_general(act[...], g[...], over_rows, preferred_element_type=jnp.float32)
    head_row[...] = msg[0:1, :]
    batch, cap = advantages.shape
    for m in range(batch):
        advantages[m : m + 1, :] = msg[1:2, m * cap : (m + 1) * cap]


def local(hidden, rewards, counts, episode, down_weight, up_weight, head_weight):
    n_pipe = lax.axis_size("pipe")
    n_tp = lax.axis_size("tp")
    batch, cap, width = hidden.shape
    rows = batch * cap
    down, up = down_weight[0], up_weight[0]
    inner = down.shape[1]
    own = rows // n_tp
    sent = own if own % 16 == 0 else rows
    chunks = own // CHUNK
    slice_width = width // n_pipe
    block = max(slice_width, 128)
    bf16, f32 = jnp.bfloat16, jnp.float32
    vmem = pl.BlockSpec(memory_space=pltpu.VMEM)
    smem = pl.BlockSpec(memory_space=pltpu.SMEM)
    anywhere = pl.BlockSpec(memory_space=pl.ANY)
    dma = pltpu.SemaphoreType.DMA
    h, act, pg, g, msg = pl.pallas_call(
        functools.partial(kernel, n_pipe, n_tp, batch),
        out_shape=(
            jax.ShapeDtypeStruct((rows, width), bf16),
            jax.ShapeDtypeStruct((rows, inner), bf16),
            jax.ShapeDtypeStruct((rows, inner), bf16),
            jax.ShapeDtypeStruct((rows, width), bf16),
            jax.ShapeDtypeStruct((8, block), f32),
        ),
        in_specs=[anywhere, vmem, smem, vmem, anywhere, anywhere, vmem],
        out_specs=(anywhere, anywhere, anywhere, anywhere, vmem),
        scratch_shapes=[
            pltpu.VMEM((n_tp, sent, width), bf16),
            pltpu.VMEM((n_tp * rows, width), bf16),
            pltpu.VMEM((rows, width), bf16),
            pltpu.VMEM((n_tp * rows, width), bf16),
            pltpu.VMEM((rows, width), bf16),
            pltpu.VMEM((2, rows, width), bf16),
            pltpu.VMEM((2, rows, inner), bf16),
            pltpu.VMEM((rows, inner), f32),
            pltpu.VMEM((rows, inner), f32),
            pltpu.VMEM((own, inner), f32),
            pltpu.VMEM((n_tp, width, inner), bf16),
            pltpu.VMEM((n_tp, inner, width), bf16),
            pltpu.VMEM((n_tp, inner, width), bf16),
            pltpu.VMEM((n_tp, width, inner), bf16),
            pltpu.VMEM((n_tp * CHUNK, width), f32),
            pltpu.VMEM((n_tp * CHUNK, width), f32),
            pltpu.VMEM((n_tp, CHUNK, width), f32),
            pltpu.VMEM((rows, 128), f32),
            pltpu.VMEM((rows, rows), f32),
            pltpu.VMEM((32, rows), f32),
            pltpu.VMEM((n_pipe, 8, block), f32),
            pltpu.VMEM((8, block), f32),
            dma((chunks, PIECES)),
            dma((chunks, PIECES)),
            dma((chunks, PIECES)),
            dma((chunks, PIECES)),
            dma((chunks, n_tp)),
            dma((chunks, n_tp)),
            dma((chunks, n_tp)),
            dma((chunks, n_tp)),
            dma((8, n_tp)),
            dma((8, n_tp)),
            dma((n_pipe,)),
            dma((1,)),
            dma((4,)),
        ],
        compiler_params=pltpu.CompilerParams(
            collective_id=0, has_side_effects=True, vmem_limit_bytes=56 * 1024 * 1024
        ),
        name="adapters",
    )(
        hidden.reshape(rows, width),
        rewards,
        counts,
        episode,
        down,
        up,
        head_weight,
    )
    tile = min(512, width)
    exact = slice_width == block

    def whole(shape):
        return pl.BlockSpec(shape, lambda b: (0, 0))

    grad_down, grad_up, head_row, advantages = pl.pallas_call(
        gradients,
        grid=(width // tile,),
        out_shape=(
            jax.ShapeDtypeStruct((width, inner), f32),
            jax.ShapeDtypeStruct((inner, width), f32),
            jax.ShapeDtypeStruct((1, block), f32),
            jax.ShapeDtypeStruct((batch, cap), f32),
        ),
        in_specs=[
            pl.BlockSpec((rows, tile), lambda b: (0, b)),
            whole((rows, inner)),
            whole((rows, inner)),
            pl.BlockSpec((rows, tile), lambda b: (0, b)),
            whole((8, block)),
        ],
        out_specs=(
            pl.BlockSpec((tile, inner), lambda b: (b, 0)),
            pl.BlockSpec((inner, tile), lambda b: (0, b)),
            whole((1, block)),
            whole((batch, cap)),
        ),
        compiler_params=pltpu.CompilerParams(vmem_limit_bytes=60 * 1024 * 1024),
        name="gradients",
    )(h, act, pg, g, msg)
    if not exact:
        offset = lax.rem(lax.axis_index("pipe") * slice_width, block)
        head_row = lax.dynamic_slice(head_row, (0, offset), (1, slice_width))
    return (grad_down[None], grad_up[None], head_row, advantages)


def solution(mesh):
    return jax.shard_map(
        local,
        mesh=mesh,
        in_specs=(
            P(None, None, "tp"),
            P(),
            P(),
            P(),
            P("pipe", "tp", None),
            P("pipe", None, "tp"),
            P("tp"),
        ),
        out_specs=(P("pipe", "tp", None), P("pipe", None, "tp"), P("tp", "pipe"), P()),
        check_vma=False,
    )
```

```python
import functools

import jax
import jax.numpy as jnp
from jax import lax
from jax.experimental import pallas as pl
from jax.experimental.pallas import tpu as pltpu
from jax.sharding import PartitionSpec as P

MESH = pl.DeviceIdType.MESH
CHUNK = 8
PIECES = 4


def derivative(pre_act):
    s = jax.nn.sigmoid(pre_act)
    return s * (1.0 + pre_act * (1.0 - s))


def kernel(
    n_pipe,
    n_tp,
    batch,
    hidden,
    rewards,
    counts,
    episode,
    down,
    up,
    head,
    h_out,
    act_out,
    pg_out,
    g_out,
    msg_out,
    hid,
    h_buf,
    o_buf,
    g_buf,
    q_buf,
    flat,
    narrow,
    act_buf,
    pg_buf,
    pre_buf,
    wd,
    wu,
    wd_t,
    wu_t,
    hd,
    o_sum,
    ghx,
    vx,
    w_buf,
    aux,
    msg,
    msg_in,
    f_send,
    f_recv,
    b_send,
    b_recv,
    gx_send,
    gx_recv,
    px_send,
    px_recv,
    x_send,
    x_recv,
    msg_send,
    msg_recv,
    local_sem,
):
    p = lax.axis_index("pipe")
    me = lax.axis_index("tp")
    last = n_pipe - 1
    is_last = p == last
    width = h_buf.shape[1]
    rows = vx.shape[0]
    inner = wd.shape[2]
    own = rows // n_tp
    chunks = own // CHUNK
    fold = CHUNK * n_tp
    piece = width // PIECES
    peers = [lax.rem(me + i, n_tp) for i in range(1, n_tp)]
    block = msg.shape[2]
    sent = hid.shape[1]
    bf16, f32 = jnp.bfloat16, jnp.float32

    def to_pipe(q):
        return {"pipe": q, "tp": me}

    def to_peer(t):
        return {"pipe": p, "tp": t}

    barrier = pltpu.get_barrier_semaphore()
    for t in peers:
        pl.semaphore_signal(barrier, inc=1, device_id=to_peer(t), device_id_type=MESH)

    @pl.when(p > 0)
    def _():
        pl.semaphore_signal(barrier, inc=1, device_id=to_pipe(p - 1), device_id_type=MESH)

    @pl.when(p < last)
    def _():
        pl.semaphore_signal(barrier, inc=1, device_id=to_pipe(p + 1), device_id_type=MESH)
        pl.semaphore_signal(barrier, inc=1, device_id=to_pipe(last), device_id_type=MESH)

    @pl.when(is_last)
    def _():
        def greet(q, carry):
            pl.semaphore_signal(barrier, inc=1, device_id=to_pipe(q), device_id_type=MESH)
            return carry

        lax.fori_loop(0, last, greet, 0)

    @pl.when(p == 0)
    def _():
        pl.semaphore_wait(barrier, n_tp + 1)

    @pl.when((p > 0) & (p < last))
    def _():
        pl.semaphore_wait(barrier, n_tp + 2)

    @pl.when(is_last)
    def _():
        pl.semaphore_wait(barrier, n_tp + last)

    def peer_copy(src, dst, kind, t, slot):
        return pltpu.make_async_remote_copy(
            src_ref=src,
            dst_ref=dst,
            send_sem=x_send.at[kind, t],
            recv_sem=x_recv.at[kind, slot],
            device_id=to_peer(t),
            device_id_type=MESH,
        )

    def head_copy(t, slot):
        rs = pl.ds(pl.multiple_of(slot * CHUNK, CHUNK), CHUNK)
        return peer_copy(hd.at[rs], hd.at[rs], 6, t, slot)

    def from_row(t):
        return pl.multiple_of(t * own, own) if sent == own else 0

    def hidden_copy(t, slot):
        return peer_copy(hidden.at[pl.ds(from_row(t), sent)], hid.at[slot], 0, t, slot)

    loads = [
        pltpu.make_async_copy(down, wd.at[me], local_sem.at[0]),
        pltpu.make_async_copy(up, wu.at[me], local_sem.at[1]),
    ]
    own_hidden = pltpu.make_async_copy(
        hidden.at[pl.ds(from_row(me), sent)], hid.at[me], local_sem.at[2]
    )

    @pl.when(p == 0)
    def _():
        own_hidden.start()
        for t in peers:
            hidden_copy(t, me).start()

    for t in peers:
        peer_copy(down, wd.at[me], 1, t, me).start()
    loads[0].start()
    for t in peers:
        peer_copy(up, wu.at[me], 2, t, me).start()
    loads[1].start()

    @pl.when(is_last)
    def _():
        hd[pl.ds(pl.multiple_of(me * CHUNK, CHUNK), CHUNK), :] = jnp.broadcast_to(
            head[...].astype(f32).reshape(1, width), (CHUNK, width)
        )
        for t in peers:
            head_copy(t, me).start()

    @pl.when(is_last)
    def _():
        shape = (rows, rows)
        i = lax.broadcasted_iota(jnp.int32, shape, 0)
        j = lax.broadcasted_iota(jnp.int32, shape, 1)
        cap = rows // batch
        for m in range(batch):
            aux[16:17, m * cap : (m + 1) * cap] = rewards[m : m + 1, :]
            aux[24:25, m * cap : (m + 1) * cap] = episode[m : m + 1, :].astype(f32)

        def per_slot(idx):
            live = jnp.zeros(shape, jnp.float32)
            next_live = jnp.zeros(shape, jnp.float32)
            owner = jnp.zeros(shape, jnp.int32)
            for m in range(batch):
                inside = (idx >= m * cap) & (idx < (m + 1) * cap)
                slot = idx - m * cap
                live = jnp.where(inside & (slot < counts[m]), 1.0, live)
                next_live = jnp.where(inside & (slot + 1 < counts[m]), 1.0, next_live)
                owner = jnp.where(inside, m, owner)
            return live, next_live, owner

        live_i, _, owner_i = per_slot(i)
        live_j, next_live_j, owner_j = per_slot(j)
        ep_j = jnp.broadcast_to(aux[24:25, :], shape)
        ep_i = jnp.broadcast_to(
            jnp.sum(jnp.where(i == j, ep_j, 0.0), axis=1, keepdims=True), shape
        )
        keep = (j >= i) & (ep_i == ep_j) & (owner_i == owner_j)
        w_buf[...] = jnp.where(keep, live_i * live_j, 0.0)
        ep_next = jnp.broadcast_to(
            jnp.sum(jnp.where(i == j + 1, ep_i, 0.0), axis=0, keepdims=True), shape
        )
        follow = jnp.where(ep_next == ep_j, next_live_j, 0.0)
        aux[0:8, :] = live_j[0:8]
        aux[8:16, :] = follow[0:8]

    @pl.when(p == 0)
    def _():
        own_hidden.wait()
        for t in peers:
            hidden_copy(t, t).wait_recv()

    loads[0].wait()
    for t in peers:
        peer_copy(down, wd.at[t], 1, t, t).wait_recv()
    loads[1].wait()
    for t in peers:
        peer_copy(up, wu.at[t], 2, t, t).wait_recv()

    def turn():
        size = min(256, width)

        def one(b, carry):
            cs = pl.ds(pl.multiple_of(b * size, size), size)
            for f in range(n_tp):
                wd_t[f, :, cs] = wd[f, cs, :].T
                wu_t[f, cs, :] = wu[f, :, cs].T
            return carry

        lax.fori_loop(0, width // size, one, 0)

    @pl.when(p >= n_pipe // 2)
    def _():
        turn()

    def short_rows(c):
        return pl.ds(pl.multiple_of(c * CHUNK, CHUNK), CHUNK)

    def global_rows(c):
        return pl.ds(pl.multiple_of(me * own + c * CHUNK, CHUNK), CHUNK)

    def out_rows(c):
        return pl.ds(pl.multiple_of(c * fold, fold), fold)

    def fold_rows(t, c):
        return pl.ds(pl.multiple_of((t * chunks + c) * fold, fold), fold)

    def cols_of(s):
        return pl.ds(s * piece, piece)

    def forward_copy(c, s, target):
        return pltpu.make_async_remote_copy(
            src_ref=o_buf.at[out_rows(c), cols_of(s)],
            dst_ref=h_buf.at[fold_rows(me, c), cols_of(s)],
            send_sem=f_send.at[c, s],
            recv_sem=f_recv.at[c, s],
            device_id=to_pipe(target),
            device_id_type=MESH,
        )

    def backward_copy(c, s, target):
        return pltpu.make_async_remote_copy(
            src_ref=q_buf.at[out_rows(c), cols_of(s)],
            dst_ref=g_buf.at[fold_rows(me, c), cols_of(s)],
            send_sem=b_send.at[c, s],
            recv_sem=b_recv.at[c, s],
            device_id=to_pipe(target),
            device_id_type=MESH,
        )

    def grad_copy(t, c, slot):
        return pltpu.make_async_remote_copy(
            src_ref=g_buf.at[fold_rows(slot, c)],
            dst_ref=g_buf.at[fold_rows(slot, c)],
            send_sem=gx_send.at[c, t],
            recv_sem=gx_recv.at[c, slot],
            device_id=to_peer(t),
            device_id_type=MESH,
        )

    def pre_grad_copy(t, c, slot):
        rs = pl.ds(pl.multiple_of(slot * own + c * CHUNK, CHUNK), CHUNK)
        return pltpu.make_async_remote_copy(
            src_ref=pg_buf.at[rs],
            dst_ref=pg_buf.at[rs],
            send_sem=px_send.at[c, t],
            recv_sem=px_recv.at[c, slot],
            device_id=to_peer(t),
            device_id_type=MESH,
        )

    def contract(x, weight, s):
        total = jnp.zeros((CHUNK, inner), f32)
        for f in range(n_tp):
            part = jnp.dot(x, weight[f, cols_of(s), :], preferred_element_type=f32)
            total += part[f * CHUNK : (f + 1) * CHUNK]
        return total

    def expand(x, weight, s):
        return jnp.concatenate(
            [
                jnp.dot(x, weight[f, :, cols_of(s)], preferred_element_type=f32)
                for f in range(n_tp)
            ],
            axis=0,
        )

    def forward(first_layer, final_layer, c, carry):
        rs = fold_rows(me, c)

        if first_layer:
            first = c * CHUNK if sent == own else me * own + c * CHUNK
            pair = pl.ds(pl.multiple_of(first // 16 * 16, 16), 16)
            odd = lax.rem(first // CHUNK, 2) == 1
            for s in range(PIECES):
                parts = []
                for f in range(n_tp):
                    both = hid[f, pair, cols_of(s)].astype(f32)
                    parts.append(jnp.where(odd, both[CHUNK:], both[:CHUNK]))
                h_buf[rs, cols_of(s)] = jnp.concatenate(parts, axis=0).astype(bf16)

        pre = jnp.zeros((CHUNK, inner), f32)
        for s in range(PIECES):

            if not first_layer:
                forward_copy(c, s, p - 1).wait_recv()

            pre += contract(h_buf[rs, cols_of(s)], wd, s)
        act = jax.nn.silu(pre).astype(bf16)
        for s in range(PIECES):
            out = h_buf[rs, cols_of(s)].astype(f32) + expand(act, wu, s)
            o_buf[out_rows(c), cols_of(s)] = out.astype(bf16)

            if not final_layer:
                forward_copy(c, s, p + 1).start()

        pre_buf[short_rows(c)] = pre
        act_buf[global_rows(c)] = act.astype(f32)

        if final_layer:
            value = jnp.zeros((fold, 1), f32)
            for s in range(PIECES):
                value += jnp.sum(
                    o_buf[out_rows(c), cols_of(s)].astype(f32) * hd[:, cols_of(s)],
                    axis=1,
                    keepdims=True,
                )
            total = value[0:CHUNK]
            for f in range(1, n_tp):
                total += value[f * CHUNK : (f + 1) * CHUNK]
            vx[global_rows(c)] = jnp.broadcast_to(total, (CHUNK, vx.shape[1]))

        return carry

    def by_place(body):
        @pl.when(p == 0)
        def _():
            lax.fori_loop(0, chunks, functools.partial(body, True, n_pipe == 1), 0)

        @pl.when((p > 0) & (p < last))
        def _():
            lax.fori_loop(0, chunks, functools.partial(body, False, False), 0)

        @pl.when((p > 0) & is_last)
        def _():
            lax.fori_loop(0, chunks, functools.partial(body, False, True), 0)

    @pl.when(is_last)
    def _():
        for t in peers:
            head_copy(t, t).wait_recv()

    by_place(forward)

    def own_rows(t):
        return pl.ds(pl.multiple_of(t * own, own), own)

    def kept_copy(t, slot):
        rs = pl.ds(pl.multiple_of(slot * chunks * fold, chunks * fold), chunks * fold)
        return peer_copy(h_buf.at[rs], h_buf.at[rs], 3, t, slot)

    def act_copy(t, slot):
        return peer_copy(act_buf.at[own_rows(slot)], act_buf.at[own_rows(slot)], 4, t, slot)

    def value_copy(t, slot):
        return peer_copy(vx.at[own_rows(slot)], vx.at[own_rows(slot)], 5, t, slot)

    @pl.when(is_last)
    def _():
        for t in peers:
            value_copy(t, me).start()
        for t in peers:
            value_copy(t, t).wait_recv()
        shape = (rows, rows)
        i = lax.broadcasted_iota(jnp.int32, shape, 0)
        j = lax.broadcasted_iota(jnp.int32, shape, 1)
        value = jnp.broadcast_to(vx[:, 0:1], shape)
        value_row = jnp.sum(jnp.where(i == j, value, 0.0), axis=0, keepdims=True)
        next_row = jnp.sum(jnp.where(i == j + 1, value, 0.0), axis=0, keepdims=True)
        delta = (aux[16:17, :] + aux[8:9, :] * next_row - value_row) * aux[0:1, :]
        adv = jnp.sum(w_buf[...] * delta, axis=1, keepdims=True)
        adv_all = jnp.broadcast_to(adv, shape)
        w_buf[...] = adv_all
        aux[0:8, :] = jnp.broadcast_to(
            jnp.sum(jnp.where(i == j, adv_all, 0.0), axis=0, keepdims=True), (8, rows)
        )

    for t in peers:
        kept_copy(t, me).start()
        act_copy(t, me).start()

    @pl.when(p < n_pipe // 2)
    def _():
        turn()

    def signed_grad(c):
        grad = -w_buf[global_rows(c), 0:1]
        return jnp.concatenate([grad] * n_tp, axis=0)

    def backward(first_layer, final_layer, c, carry):
        rs = fold_rows(me, c)

        if final_layer:
            grad = signed_grad(c)
            for s in range(PIECES):
                g_buf[rs, cols_of(s)] = (grad * hd[:, cols_of(s)]).astype(bf16)

        total = jnp.zeros((CHUNK, inner), f32)
        for s in range(PIECES):

            if not final_layer:
                backward_copy(c, s, p + 1).wait_recv()

            total += contract(g_buf[rs, cols_of(s)], wu_t, s)
        pg = (total * derivative(pre_buf[short_rows(c)])).astype(bf16)

        if not first_layer:
            for s in range(PIECES):
                out = g_buf[rs, cols_of(s)].astype(f32) + expand(pg, wd_t, s)
                q_buf[out_rows(c), cols_of(s)] = out.astype(bf16)
                backward_copy(c, s, p - 1).start()

        pg_buf[global_rows(c)] = pg.astype(f32)
        for t in peers:
            grad_copy(t, c, me).start()
            pre_grad_copy(t, c, me).start()
        return carry

    def unfold(buf, k):
        parts = []
        for half in range(2):
            start = pl.multiple_of((2 * k + half) * fold, fold)
            both = buf[pl.ds(start, fold)].astype(f32)
            mine = both[0:CHUNK]
            for f in range(1, n_tp):
                mine = jnp.where(me == f, both[f * CHUNK : (f + 1) * CHUNK], mine)
            parts.append(mine)
        return jnp.concatenate(parts, axis=0).astype(bf16)

    def flat_pass(buf, index):
        def one(k, carry):
            flat[index, pl.ds(pl.multiple_of(k * 16, 16), 16)] = unfold(buf, k)
            return carry

        lax.fori_loop(0, rows // 16, one, 0)

    def keep():
        for t in peers:
            kept_copy(t, t).wait_recv()
            act_copy(t, t).wait_recv()
        flat_pass(h_buf, 0)
        narrow[0] = act_buf[...].astype(bf16)
        copies[0].start()
        copies[1].start()

    copies = [
        pltpu.make_async_copy(flat.at[0], h_out, local_sem.at[0]),
        pltpu.make_async_copy(narrow.at[0], act_out, local_sem.at[1]),
        pltpu.make_async_copy(flat.at[1], g_out, local_sem.at[2]),
        pltpu.make_async_copy(narrow.at[1], pg_out, local_sem.at[3]),
    ]

    @pl.when(p < last)
    def _():
        keep()

    by_place(backward)

    @pl.when(is_last)
    def _():
        keep()

    def gather(c, carry):
        for t in peers:
            grad_copy(t, c, t).wait_recv()
            pre_grad_copy(t, c, t).wait_recv()
        return carry

    lax.fori_loop(0, chunks, gather, 0)
    flat_pass(g_buf, 1)
    narrow[1] = pg_buf[...].astype(bf16)
    copies[2].start()
    copies[3].start()

    slice_width = width // n_pipe

    def message_copy(q):
        return pltpu.make_async_remote_copy(
            src_ref=msg.at[q],
            dst_ref=msg_in,
            send_sem=msg_send.at[q],
            recv_sem=msg_recv.at[0],
            device_id=to_pipe(q),
            device_id_type=MESH,
        )

    def head_rows(t):
        return pl.ds(pl.multiple_of(t * CHUNK, CHUNK), CHUNK)

    def head_grad_copy(t, slot):
        return peer_copy(o_sum.at[head_rows(t)], ghx.at[slot], 7, t, slot)

    @pl.when(is_last)
    def _():
        for s in range(PIECES):
            acc = jnp.zeros((fold, piece), f32)
            for c in range(chunks):
                acc += o_buf[out_rows(c), cols_of(s)].astype(f32) * signed_grad(c)
            o_sum[:, cols_of(s)] = acc
        ghx[me] = o_sum[head_rows(me)]
        for t in peers:
            head_grad_copy(t, me).start()
        for t in peers:
            head_grad_copy(t, t).wait_recv()
        adv_row = aux[0:1, :]
        for b in range(width // block):
            cs = pl.ds(b * block, block)
            acc = ghx[0, :, cs]
            for t in range(1, n_tp):
                acc += ghx[t, :, cs]
            head_grad = jnp.sum(acc, axis=0, keepdims=True)
            for q in range(n_pipe):
                if q * slice_width // block == b:
                    msg[q, 0:1, :] = head_grad
                    msg[q, 1:2, 0:rows] = adv_row
        for q in range(last):
            message_copy(q).start()
        msg_out[...] = msg[last]

    @pl.when(p < last)
    def _():
        message_copy(last).wait_recv()
        msg_out[...] = msg_in[...]

    def finish(c, carry):
        for s in range(PIECES):

            @pl.when(p < last)
            def _():
                forward_copy(c, s, p + 1).wait_send()

            @pl.when(p > 0)
            def _():
                backward_copy(c, s, p - 1).wait_send()

        for t in peers:
            grad_copy(t, c, me).wait_send()
            pre_grad_copy(t, c, me).wait_send()
        return carry

    lax.fori_loop(0, chunks, finish, 0)

    @pl.when(p == 0)
    def _():
        for t in peers:
            hidden_copy(t, me).wait_send()

    for t in peers:
        peer_copy(down, wd.at[me], 1, t, me).wait_send()
        peer_copy(up, wu.at[me], 2, t, me).wait_send()
        kept_copy(t, me).wait_send()
        act_copy(t, me).wait_send()

    @pl.when(is_last)
    def _():
        for t in peers:
            head_copy(t, me).wait_send()
            value_copy(t, me).wait_send()
            head_grad_copy(t, me).wait_send()
        for q in range(last):
            message_copy(q).wait_send()

    for copy in copies:
        copy.wait()


def gradients(h, act, pg, g, msg, grad_down, grad_up, head_row, advantages):
    over_rows = (((0,), (0,)), ((), ()))
    grad_down[...] = lax.dot_general(
        h[...], pg[...], over_rows, preferred_element_type=jnp.float32
    )
    grad_up[...] = lax.dot_general(act[...], g[...], over_rows, preferred_element_type=jnp.float32)
    head_row[...] = msg[0:1, :]
    batch, cap = advantages.shape
    for m in range(batch):
        advantages[m : m + 1, :] = msg[1:2, m * cap : (m + 1) * cap]


def local(hidden, rewards, counts, episode, down_weight, up_weight, head_weight):
    n_pipe = lax.axis_size("pipe")
    n_tp = lax.axis_size("tp")
    batch, cap, width = hidden.shape
    rows = batch * cap
    down, up = down_weight[0], up_weight[0]
    inner = down.shape[1]
    own = rows // n_tp
    sent = own if own % 16 == 0 else rows
    chunks = own // CHUNK
    slice_width = width // n_pipe
    block = max(slice_width, 128)
    bf16, f32 = jnp.bfloat16, jnp.float32
    vmem = pl.BlockSpec(memory_space=pltpu.VMEM)
    smem = pl.BlockSpec(memory_space=pltpu.SMEM)
    anywhere = pl.BlockSpec(memory_space=pl.ANY)
    dma = pltpu.SemaphoreType.DMA
    h, act, pg, g, msg = pl.pallas_call(
        functools.partial(kernel, n_pipe, n_tp, batch),
        out_shape=(
            jax.ShapeDtypeStruct((rows, width), bf16),
            jax.ShapeDtypeStruct((rows, inner), bf16),
            jax.ShapeDtypeStruct((rows, inner), bf16),
            jax.ShapeDtypeStruct((rows, width), bf16),
            jax.ShapeDtypeStruct((8, block), f32),
        ),
        in_specs=[anywhere, vmem, smem, vmem, anywhere, anywhere, vmem],
        out_specs=(anywhere, anywhere, anywhere, anywhere, vmem),
        scratch_shapes=[
            pltpu.VMEM((n_tp, sent, width), bf16),
            pltpu.VMEM((n_tp * rows, width), bf16),
            pltpu.VMEM((rows, width), bf16),
            pltpu.VMEM((n_tp * rows, width), bf16),
            pltpu.VMEM((rows, width), bf16),
            pltpu.VMEM((2, rows, width), bf16),
            pltpu.VMEM((2, rows, inner), bf16),
            pltpu.VMEM((rows, inner), f32),
            pltpu.VMEM((rows, inner), f32),
            pltpu.VMEM((own, inner), f32),
            pltpu.VMEM((n_tp, width, inner), bf16),
            pltpu.VMEM((n_tp, inner, width), bf16),
            pltpu.VMEM((n_tp, inner, width), bf16),
            pltpu.VMEM((n_tp, width, inner), bf16),
            pltpu.VMEM((n_tp * CHUNK, width), f32),
            pltpu.VMEM((n_tp * CHUNK, width), f32),
            pltpu.VMEM((n_tp, CHUNK, width), f32),
            pltpu.VMEM((rows, 128), f32),
            pltpu.VMEM((rows, rows), f32),
            pltpu.VMEM((32, rows), f32),
            pltpu.VMEM((n_pipe, 8, block), f32),
            pltpu.VMEM((8, block), f32),
            dma((chunks, PIECES)),
            dma((chunks, PIECES)),
            dma((chunks, PIECES)),
            dma((chunks, PIECES)),
            dma((chunks, n_tp)),
            dma((chunks, n_tp)),
            dma((chunks, n_tp)),
            dma((chunks, n_tp)),
            dma((8, n_tp)),
            dma((8, n_tp)),
            dma((n_pipe,)),
            dma((1,)),
            dma((4,)),
        ],
        compiler_params=pltpu.CompilerParams(
            collective_id=0, has_side_effects=True, vmem_limit_bytes=56 * 1024 * 1024
        ),
        name="adapters",
    )(
        hidden.reshape(rows, width),
        rewards,
        counts,
        episode,
        down,
        up,
        head_weight,
    )
    tile = min(1024, width)
    exact = slice_width == block

    def whole(shape):
        return pl.BlockSpec(shape, lambda b: (0, 0))

    grad_down, grad_up, head_row, advantages = pl.pallas_call(
        gradients,
        grid=(width // tile,),
        out_shape=(
            jax.ShapeDtypeStruct((width, inner), f32),
            jax.ShapeDtypeStruct((inner, width), f32),
            jax.ShapeDtypeStruct((1, block), f32),
            jax.ShapeDtypeStruct((batch, cap), f32),
        ),
        in_specs=[
            pl.BlockSpec((rows, tile), lambda b: (0, b)),
            whole((rows, inner)),
            whole((rows, inner)),
            pl.BlockSpec((rows, tile), lambda b: (0, b)),
            whole((8, block)),
        ],
        out_specs=(
            pl.BlockSpec((tile, inner), lambda b: (b, 0)),
            pl.BlockSpec((inner, tile), lambda b: (0, b)),
            whole((1, block)),
            whole((batch, cap)),
        ),
        compiler_params=pltpu.CompilerParams(vmem_limit_bytes=60 * 1024 * 1024),
        name="gradients",
    )(h, act, pg, g, msg)
    if not exact:
        offset = lax.rem(lax.axis_index("pipe") * slice_width, block)
        head_row = lax.dynamic_slice(head_row, (0, offset), (1, slice_width))
    return (grad_down[None], grad_up[None], head_row, advantages)


def solution(mesh):
    return jax.shard_map(
        local,
        mesh=mesh,
        in_specs=(
            P(None, None, "tp"),
            P(),
            P(),
            P(),
            P("pipe", "tp", None),
            P("pipe", None, "tp"),
            P("tp"),
        ),
        out_specs=(P("pipe", "tp", None), P("pipe", None, "tp"), P("tp", "pipe"), P()),
        check_vma=False,
    )
```
